256 devices in a mesh: blk: 32 (over x_hi, z, core), head: 8 (over x_lo, y).
Axes of the slice: x: 4 (x_hi: 2, x_lo: 2; x = x_hi * 2 + x_lo), y: 4, z: 8, core: 2. Of those that a mesh axis runs over, the one named last changes fastest.
Arguments:
- queries: bfloat16 [16384, 3072], P(('blk', 'head')), may hold values from -80 to 80
- keys: bfloat16 [16384, 3072], P(('blk', 'head')), may hold values from -9 to 9
- values: bfloat16 [16384, 3072], P(('blk', 'head')), may hold values from -6 to 6
- tile_mask: int32 [24, 128, 128], P('head', 'blk'), may hold values from 0 to 1, as said below
- out_weight: bfloat16 [3072, 3072], P('head'), may hold values from -0.109375 to 0.109375
Outputs:
- mixed: bfloat16 [16384, 3072], P(('blk', 'head'))
The draws below stay inside these ranges and needn't reach their ends.
Inputs may be any that keep to these rules, and one draw needn't show every extreme that they name: `tile_mask`: every diagonal entry is 1.
All inputs are finite; a program needn't handle non-finite values.
Results may differ from the reference program's by a relative error of at most 0.014.
Values may be sent and summed in bfloat16 or wider, within the bound.
A program may use at most 192 MiB of HBM per device.

```python
import math
import jax
import jax.numpy as jnp
from jax import lax

HEADS = 24
HEAD_DIM = 128
TILE = 128
TILES_FRAME = 8
TOK_BLK = 512
D = 3072
TOKENS = 16384


def base_keys(key, spread, tie):
    raw = jnp.clip(jax.random.normal(key, (TOKENS, HEADS * HEAD_DIM), jnp.float32), -4.0, 4.0)
    picked = jax.random.randint(jax.random.fold_in(key, 1), (TOKENS,), 0, 64) == 0
    nudge = jax.random.normal(jax.random.fold_in(key, 2), (TOKENS, HEADS * HEAD_DIM), jnp.float32)
    follow = jnp.roll(picked, 1)
    twin = jnp.roll(raw, 1, axis=0) + 0.012 * nudge
    raw = jnp.where((follow & (tie > 0))[:, None], twin, raw)
    level = jnp.exp(spread * jax.random.uniform(jax.random.fold_in(key, 3), (TOKENS, 1), jnp.float32, -1.0, 1.0))
    level = jnp.where((picked | follow)[:, None], 1.0, level)
    return raw * level


def draw_keys(key, part):
    result = base_keys(key, 0.0, 0)
    return result.astype(jnp.bfloat16)


def draw_queries(key, part):
    key = jax.random.fold_in(key, 7)
    own = jnp.clip(jax.random.normal(key, (TOKENS, HEADS * HEAD_DIM), jnp.float32), -4.0, 4.0)
    return own.astype(jnp.bfloat16)


def draw_tile_mask(key, part):
    key = jax.random.fold_in(key, 11)
    tile_total = TOKENS // TILE
    frame_total = tile_total // TILES_FRAME
    reach = jax.random.randint(jax.random.fold_in(key, 1), (HEADS, 1, 1), TILES_FRAME // 2, TILES_FRAME + frame_total)
    extra = jax.random.randint(jax.random.fold_in(key, 2), (HEADS, tile_total, tile_total), 0, 16)
    tile_ids = jnp.arange(tile_total, dtype=jnp.int32)
    frames = tile_ids // TILES_FRAME
    places = tile_ids % TILES_FRAME
    distance = jnp.abs(places[:, None] - places[None, :]) + jnp.abs(frames[:, None] - frames[None, :])
    allowed = (distance[None, :, :] <= reach) | (extra == 0)
    return allowed.astype(jnp.int32)


def block_scale(key, extent, cuts, least, top_value):
    loudness, own = 1.0, jax.random.fold_in(key, 6)
    for position, parts in cuts:
        steps = jnp.exp(jax.random.uniform(jax.random.fold_in(own, position), (parts,), jnp.float32, least / len(cuts), top_value / len(cuts)))
        loudness = loudness * jnp.repeat(steps, extent[position] // parts).reshape([-1 if axis == position else 1 for axis in range(len(extent))])
    return loudness


def scatter_about(key, dims, scale, limit, shards=(), held_as=jnp.bfloat16):
    entries = scale * jax.random.normal(key, dims, jnp.float32)
    if shards:
        entries = entries * block_scale(key, dims, shards, -0.22, 0.18)
    return jnp.clip(entries, -limit, limit).astype(held_as)


def setup_inputs(seed: int = 0) -> dict:
    splits = jax.random.split(jax.random.key(seed), 6)
    return {
        "queries": draw_queries(jax.random.fold_in(splits[5], 71), 0),
        "keys": draw_keys(jax.random.fold_in(splits[5], 71), 0),
        "values": scatter_about(splits[2], (TOKENS, D), 1.0, 6.0, ((0, 256),)),
        "tile_mask": draw_tile_mask(jax.random.fold_in(splits[5], 71), 0),
        "out_weight": scatter_about(splits[4], (D, D), D ** -0.5, 0.109375, ((0, 8),)),
    }


def reference(queries, keys, values, tile_mask, out_weight):
    score_scale = 1.0 / math.sqrt(HEAD_DIM)
    tiles_block = TOK_BLK // TILE
    block_count = TOKENS // TOK_BLK

    def one_head(head_index):
        query_head = lax.dynamic_slice_in_dim(queries, head_index * HEAD_DIM, HEAD_DIM, 1)
        key_head = lax.dynamic_slice_in_dim(keys, head_index * HEAD_DIM, HEAD_DIM, 1)
        value_head = lax.dynamic_slice_in_dim(values, head_index * HEAD_DIM, HEAD_DIM, 1)
        mask_head = lax.dynamic_index_in_dim(tile_mask, head_index, 0, keepdims=False)

        def one_block(block_index):
            query_block = lax.dynamic_slice_in_dim(query_head, block_index * TOK_BLK, TOK_BLK, 0)
            mask_rows = lax.dynamic_slice_in_dim(mask_head, block_index * tiles_block, tiles_block, 0)
            allowed = jnp.repeat(jnp.repeat(mask_rows, TILE, axis=0), TILE, axis=1) > 0
            scores = jnp.dot(query_block, key_head.T, preferred_element_type=jnp.float32) * score_scale
            scores = jnp.where(allowed, scores, -1e+30)
            row_top = lax.optimization_barrier(jnp.max(scores, axis=1, keepdims=True))
            raw_weights = jnp.where(allowed, jnp.exp(scores - row_top), 0.0)
            row_total = lax.optimization_barrier(jnp.sum(raw_weights, axis=1, keepdims=True))
            weighted = jnp.dot(raw_weights.astype(jnp.bfloat16), value_head, preferred_element_type=jnp.float32)
            return (weighted / row_total).astype(jnp.bfloat16)
        return lax.map(one_block, jnp.arange(block_count, dtype=jnp.int32))
    per_head = lax.map(one_head, jnp.arange(HEADS, dtype=jnp.int32))
    attention = per_head.transpose(1, 2, 0, 3).reshape(TOKENS, HEADS * HEAD_DIM)
    return jnp.dot(attention, out_weight, preferred_element_type=jnp.float32).astype(jnp.bfloat16)
```

```python
import functools
import math

import jax
import jax.numpy as jnp
from jax import lax
from jax.experimental import pallas as pl
from jax.experimental.pallas import tpu as pltpu
from jax.sharding import PartitionSpec as P

HEAD_DIM = 128
TILE = 128
MESH = pl.DeviceIdType.MESH
TO_LOG2 = math.log2(math.e) / math.sqrt(HEAD_DIM)
LOW = -1e30
BLOCKED = 2e30
VMEM_LIMIT = 60 * 2**20
NX, NY, NZ = 2, 4, 8


def place():
    blk, head = lax.axis_index("blk"), lax.axis_index("head")
    return blk // 16, (blk // 2) % NZ, blk % 2, head // NY, head % NY


def at(x_hi, z, core, x_lo, y):
    return (x_hi * 16 + z * 2 + core, x_lo * NY + y)


def greet(peers):
    barrier = pltpu.get_barrier_semaphore()
    for peer in peers:
        pl.semaphore_signal(barrier, inc=1, device_id=peer, device_id_type=MESH)
    pl.semaphore_wait(barrier, len(peers))


class Wires:
    def __init__(self, send_sems, recv_sems, local_sems):
        self.send_sems, self.recv_sems, self.local_sems = send_sems, recv_sems, local_sems
        self.used, self.used_local = 0, 0
        self.sent = []

    def push(self, src, dst, peer, land=None):
        copy = pltpu.make_async_remote_copy(
            src_ref=src,
            dst_ref=dst,
            send_sem=self.send_sems.at[self.used],
            recv_sem=self.recv_sems.at[self.used],
            device_id=peer,
            device_id_type=MESH,
        )
        arrival = copy
        if land is not None:
            arrival = pltpu.make_async_remote_copy(
                src_ref=land,
                dst_ref=land,
                send_sem=self.send_sems.at[self.used],
                recv_sem=self.recv_sems.at[self.used],
                device_id=peer,
                device_id_type=MESH,
            )
        self.used += 1
        copy.start()
        self.sent.append(copy)
        return arrival

    def local(self, src, dst):
        copy = pltpu.make_async_copy(src, dst, self.local_sems.at[self.used_local])
        self.used_local += 1
        copy.start()
        return copy

    def finish(self):
        for copy in self.sent:
            copy.wait_send()


def spread_kernel(q, k, v, m, w, q_all, k_all, v_all, m_all, w_all, send_sems, recv_sems, local_sems):
    x_hi, z, core, x_lo, y = place()
    rows = q.shape[0]
    width = q_all.shape[2]
    group = x_lo * NY + y
    other_hi, other_core, other_lo = 1 - x_hi, 1 - core, 1 - x_lo
    slot = x_hi * 2 + core
    sibling = at(x_hi, z, other_core, x_lo, y)
    across = at(other_hi, z, core, x_lo, y)
    diagonal = at(other_hi, z, other_core, x_lo, y)
    z_up, z_down = (z + 1) % NZ, (z + NZ - 1) % NZ
    up, down = at(x_hi, z_up, core, x_lo, y), at(x_hi, z_down, core, x_lo, y)
    y_up, y_down, y_far = (y + 1) % NY, (y + NY - 1) % NY, (y + 2) % NY
    partner = at(x_hi, z, core, other_lo, y)
    outer = at(other_hi, z, core, other_lo, y)
    blk = x_hi * 16 + z * 2 + core
    head_peers = [(group + step) % 8 for step in range(1, 8)]
    greet([(blk, peer) for peer in head_peers] + [sibling, across, diagonal, up, down, outer])
    wires = Wires(send_sems, recv_sems, local_sems)

    def exchange(src, dst_slot):
        arrivals = []
        for step in range(1, 8):
            peer = (group + step) % 8
            origin = (group + 8 - step) % 8
            arrivals.append(
                wires.push(
                    src.at[:, pl.ds(pl.multiple_of(peer * width, 128), width)],
                    dst_slot.at[pl.ds(pl.multiple_of(group * rows, 64), rows), :],
                    (blk, peer),
                    dst_slot.at[pl.ds(pl.multiple_of(origin * rows, 64), rows), :],
                )
            )
        own = wires.local(
            src.at[:, pl.ds(pl.multiple_of(group * width, 128), width)],
            dst_slot.at[pl.ds(pl.multiple_of(group * rows, 64), rows), :],
        )
        return arrivals, own

    def settle(pending):
        for arrival in pending[0]:
            arrival.wait_recv()
        pending[1].wait()

    k_wait = exchange(k, k_all.at[z])
    v_wait = exchange(v, v_all.at[z])
    q_wait = exchange(q, q_all.at[slot])
    m_wait = [
        wires.push(m, m_all.at[slot], sibling, m_all.at[x_hi * 2 + other_core]),
        wires.push(m, m_all.at[slot], across, m_all.at[other_hi * 2 + core]),
        wires.push(m, m_all.at[slot], diagonal, m_all.at[other_hi * 2 + other_core]),
    ]
    m_own = wires.local(m, m_all.at[slot])
    w_own = wires.local(w, w_all.at[group])

    def ring_step(full, step, direction):
        if direction > 0:
            held = (z + NZ - step) % NZ
            landing = (z + NZ - step - 1) % NZ
            return wires.push(full.at[held], full.at[held], up, full.at[landing])
        held = (z + step) % NZ
        landing = (z + step + 1) % NZ
        return wires.push(full.at[held], full.at[held], down, full.at[landing])

    settle(k_wait)
    ring = {}
    ring["ku"] = ring_step(k_all, 0, 1)
    ring["kd"] = ring_step(k_all, 0, -1)
    settle(v_wait)
    ring["vu"] = ring_step(v_all, 0, 1)
    ring["vd"] = ring_step(v_all, 0, -1)

    depth = w.shape[0]
    half = depth // 2
    columns = w.shape[1] // 2
    mine = pl.ds(pl.multiple_of(core * columns, 128), columns)
    theirs = pl.ds(pl.multiple_of(other_core * columns, 128), columns)
    top, bottom = pl.ds(0, half), pl.ds(half, half)

    def w_part(lo, yy, part, cols):
        return w_all.at[lo * NY + yy, part, cols]

    whole = pl.ds(0, depth)
    w_up = wires.push(w.at[:, mine], w_part(x_lo, y, whole, mine), (blk, x_lo * NY + y_up), w_part(x_lo, y_down, whole, mine))
    w_down = wires.push(w.at[:, mine], w_part(x_lo, y, whole, mine), (blk, x_lo * NY + y_down), w_part(x_lo, y_up, whole, mine))

    def w_cross(yy):
        return (
            wires.push(w_part(x_lo, yy, top, mine), w_part(x_lo, yy, top, mine), partner, w_part(other_lo, yy, top, mine)),
            wires.push(w_part(x_lo, yy, bottom, mine), w_part(x_lo, yy, bottom, mine), outer, w_part(other_lo, yy, bottom, mine)),
        )

    tail = []

    def w_swap(lo, yy, part):
        tail.append(wires.push(w_part(lo, yy, part, mine), w_part(lo, yy, part, mine), sibling, w_part(lo, yy, part, theirs)))

    settle(q_wait)
    tail.append(wires.push(q_all.at[slot], q_all.at[slot], sibling, q_all.at[x_hi * 2 + other_core]))
    q_across = wires.push(q_all.at[slot], q_all.at[slot], across, q_all.at[other_hi * 2 + core])
    w_own.wait()
    crossing = [w_cross(y)]

    q_across.wait_recv()
    tail.append(
        wires.push(
            q_all.at[other_hi * 2 + core],
            q_all.at[other_hi * 2 + core],
            sibling,
            q_all.at[other_hi * 2 + other_core],
        )
    )

    def ring_turn(step):
        for key, full in (("k", k_all), ("v", v_all)):
            for tag, direction in (("u", 1), ("d", -1)):
                name = key + tag
                if name not in ring:
                    continue
                ring[name].wait_recv()
                last = 4 if name in ("ku", "vd") else 3
                if step < last:
                    ring[name] = ring_step(full, step, direction)
                else:
                    del ring[name]

    ring_turn(1)
    w_up.wait_recv()
    w_far_up = wires.push(
        w_part(x_lo, y_down, top, mine), w_part(x_lo, y_down, top, mine), (blk, x_lo * NY + y_up), w_part(x_lo, y_far, top, mine)
    )
    crossing.append(w_cross(y_down))
    w_swap(x_lo, y_down, whole)
    w_down.wait_recv()
    w_far_down = wires.push(
        w_part(x_lo, y_up, bottom, mine), w_part(x_lo, y_up, bottom, mine), (blk, x_lo * NY + y_down), w_part(x_lo, y_far, bottom, mine)
    )
    crossing.append(w_cross(y_up))
    w_swap(x_lo, y_up, whole)

    def crossed(index, yy):
        crossing[index][0].wait_recv()
        w_swap(other_lo, yy, top)
        crossing[index][1].wait_recv()
        w_swap(other_lo, yy, bottom)

    crossed(0, y)
    ring_turn(2)
    w_far_up.wait_recv()
    w_far_down.wait_recv()
    crossing.append(w_cross(y_far))
    w_swap(x_lo, y_far, whole)
    crossed(1, y_down)
    crossed(2, y_up)
    ring_turn(3)
    crossed(3, y_far)
    ring_turn(4)
    for arrival in tail + m_wait:
        arrival.wait_recv()
    m_own.wait()
    wires.finish()


def spread(q, k, v, m, w):
    rows = q.shape[0]
    width = q.shape[1] // 8
    slab = rows * 8
    hbm = pl.BlockSpec(memory_space=pl.ANY)
    return pl.pallas_call(
        spread_kernel,
        out_shape=[
            jax.ShapeDtypeStruct((4, slab, width), q.dtype),
            jax.ShapeDtypeStruct((NZ, slab, width), k.dtype),
            jax.ShapeDtypeStruct((NZ, slab, width), v.dtype),
            jax.ShapeDtypeStruct((4,) + m.shape, m.dtype),
            jax.ShapeDtypeStruct((8,) + w.shape, w.dtype),
        ],
        in_specs=[hbm] * 5,
        out_specs=[hbm] * 5,
        scratch_shapes=[
            pltpu.SemaphoreType.DMA((80,)),
            pltpu.SemaphoreType.DMA((80,)),
            pltpu.SemaphoreType.DMA((8,)),
        ],
        name="spread",
        compiler_params=pltpu.CompilerParams(collective_id=1, has_side_effects=True),
    )(q, k, v, m, w)


def attend_kernel(bias, q_ref, k_ref, v_ref, o_ref, stat_ref, acc, v_turned):
    heads = bias.shape[0]
    q_count, k_count = q_ref.shape[0], k_ref.shape[0]
    step_keys = 512
    steps = k_count // step_keys
    tiles = step_keys // TILE
    slots, slot_rows = o_ref.shape[0], o_ref.shape[2]
    stat_ref[...] = jnp.zeros_like(stat_ref)
    ones = jnp.ones((16, step_keys), jnp.bfloat16)

    for head in range(heads):
        lanes = pl.ds(head * HEAD_DIM, HEAD_DIM)

        def turn(i, unused):
            at_keys = pl.ds(pl.multiple_of(i * step_keys, step_keys), step_keys)
            v_turned[:, at_keys] = v_ref[at_keys, lanes].T
            return unused

        lax.fori_loop(0, steps, turn, 0)
        scaled = q_ref[:, lanes].astype(jnp.float32) * TO_LOG2
        coarse = scaled.astype(jnp.bfloat16)
        fine = (scaled - coarse.astype(jnp.float32)).astype(jnp.bfloat16)
        query = jnp.concatenate([coarse, fine], axis=1)
        acc[...] = jnp.zeros_like(acc)

        def step(i, carry):
            top, total = carry
            at_keys = pl.ds(pl.multiple_of(i * step_keys, step_keys), step_keys)
            key = k_ref[at_keys, lanes]
            scores = lax.dot_general(
                jnp.concatenate([key, key], axis=1),
                query,
                (((1,), (1,)), ((), ())),
                preferred_element_type=jnp.float32,
            )
            blocked = [bias[head, pl.ds(i * tiles + a, 1), :] for a in range(tiles)]
            next_top = top
            for a in range(tiles):
                tile_top = jnp.max(scores[a * TILE : (a + 1) * TILE], axis=0, keepdims=True)
                next_top = jnp.maximum(next_top, tile_top - blocked[a])
            weights = jnp.concatenate(
                [
                    jnp.exp2(scores[a * TILE : (a + 1) * TILE] - (next_top + blocked[a])).astype(jnp.bfloat16)
                    for a in range(tiles)
                ],
                axis=0,
            )
            shrink = jnp.exp2(top - next_top)
            added = lax.dot_general(
                jnp.concatenate([v_turned[:, at_keys], ones], axis=0),
                weights,
                (((1,), (0,)), ((), ())),
                preferred_element_type=jnp.float32,
            )
            acc[...] = acc[...] * shrink + added[:HEAD_DIM]
            return next_top, total * shrink + added[HEAD_DIM : HEAD_DIM + 1]

        start = (jnp.full((1, q_count), LOW, jnp.float32), jnp.zeros((1, q_count), jnp.float32))
        top, total = lax.fori_loop(0, steps, step, start, unroll=2)
        mean = (acc[...] / jnp.maximum(total, 1e-30)).astype(jnp.bfloat16)
        for s in range(slots):
            cols = slice(s * slot_rows, (s + 1) * slot_rows)
            o_ref[s, head * HEAD_DIM : (head + 1) * HEAD_DIM, :] = mean[:, cols]
            stat_ref[s, head : head + 1, :] = top[:, cols]
            stat_ref[s, 3 + head : 4 + head, :] = total[:, cols]


def attend(bias, q_all, k_all, v_all):
    slots, slab, width = q_all.shape
    vmem = pl.BlockSpec(memory_space=pltpu.VMEM)
    q_count, k_count = slots * slab, k_all.shape[0] * slab
    return pl.pallas_call(
        attend_kernel,
        out_shape=[
            jax.ShapeDtypeStruct((slots, width, slab), jnp.bfloat16),
            jax.ShapeDtypeStruct((slots, 8, slab), jnp.float32),
        ],
        in_specs=[vmem] * 4,
        out_specs=[vmem] * 2,
        scratch_shapes=[
            pltpu.VMEM((HEAD_DIM, q_count), jnp.float32),
            pltpu.VMEM((HEAD_DIM, k_count), jnp.bfloat16),
        ],
        name="attend",
        compiler_params=pltpu.CompilerParams(vmem_limit_bytes=VMEM_LIMIT),
    )(bias, q_all.reshape(q_count, width), k_all.reshape(k_count, width), v_all.reshape(k_count, width))


def merge_kernel(o, stat, w, out, o_in, stat_in, mixed_in, ready, w_here, send_sems, recv_sems, local_sems):
    x_hi, z, core, x_lo, y = place()
    group = x_lo * NY + y
    other_hi, other_core = 1 - x_hi, 1 - core
    slot = x_hi * 2 + core
    blk = x_hi * 16 + z * 2 + core
    rows = out.shape[0]
    heads = 3
    wires = Wires(send_sems, recv_sems, local_sems)
    w_loads = [wires.local(w.at[g], w_here.at[g]) for g in range(8)]
    others = [(other_hi, core), (other_hi, other_core), (x_hi, other_core)]
    greet(
        [(blk, (group + step) % 8) for step in range(1, 8)]
        + [at(hi, z, c, x_lo, y) for hi, c in others]
    )
    arrivals = []
    for hi, c in others:
        peer_slot, peer = hi * 2 + c, at(hi, z, c, x_lo, y)
        arrivals.append(wires.push(o.at[peer_slot], o_in.at[slot], peer, o_in.at[peer_slot]))
        arrivals.append(wires.push(stat.at[peer_slot], stat_in.at[slot], peer, stat_in.at[peer_slot]))
    for arrival in arrivals:
        arrival.wait_recv()
    o_in[slot] = o[slot]
    stat_in[slot] = stat[slot]
    slots = o_in.shape[0]
    for head in range(heads):
        tops = [stat_in[s, head : head + 1, :] for s in range(slots)]
        best = functools.reduce(jnp.maximum, tops)
        shares = [stat_in[s, 3 + head : 4 + head, :] * jnp.exp2(tops[s] - best) for s in range(slots)]
        total = functools.reduce(jnp.add, shares)
        band = slice(head * HEAD_DIM, (head + 1) * HEAD_DIM)
        blend = functools.reduce(
            jnp.add,
            [o_in[s, band, :].astype(jnp.float32) * (shares[s] / total) for s in range(slots)],
        )
        ready[:, band] = blend.T.astype(jnp.bfloat16)
    pieces = []
    for step in range(1, 8):
        peer = (group + step) % 8
        origin = (group + 8 - step) % 8
        pieces.append(
            wires.push(
                ready.at[pl.ds(pl.multiple_of(peer * rows, 64), rows), :],
                mixed_in.at[group],
                (blk, peer),
                mixed_in.at[origin],
            )
        )
    mixed_in[group] = ready[pl.ds(pl.multiple_of(group * rows, 64), rows), :]
    for piece in pieces:
        piece.wait_recv()
    for load in w_loads:
        load.wait()
    cols = 768
    for c in range(out.shape[1] // cols):
        total = jnp.zeros((rows, cols), jnp.float32)
        for g in range(8):
            total += jnp.dot(
                mixed_in[g], w_here[g, :, c * cols : (c + 1) * cols], preferred_element_type=jnp.float32
            )
        out[:, c * cols : (c + 1) * cols] = total.astype(jnp.bfloat16)
    wires.finish()


def merge(o, stat, w_all, rows):
    slots, width, slab = o.shape
    vmem = pl.BlockSpec(memory_space=pltpu.VMEM)
    return pl.pallas_call(
        merge_kernel,
        out_shape=jax.ShapeDtypeStruct((rows, w_all.shape[2]), jnp.bfloat16),
        in_specs=[vmem, vmem, pl.BlockSpec(memory_space=pl.ANY)],
        out_specs=vmem,
        scratch_shapes=[
            pltpu.VMEM(o.shape, o.dtype),
            pltpu.VMEM(stat.shape, stat.dtype),
            pltpu.VMEM((8, rows, width), jnp.bfloat16),
            pltpu.VMEM((slab, width), jnp.bfloat16),
            pltpu.VMEM(w_all.shape, w_all.dtype),
            pltpu.SemaphoreType.DMA((16,)),
            pltpu.SemaphoreType.DMA((16,)),
            pltpu.SemaphoreType.DMA((8,)),
        ],
        name="merge",
        compiler_params=pltpu.CompilerParams(
            collective_id=2, has_side_effects=True, vmem_limit_bytes=VMEM_LIMIT
        ),
    )(o, stat, w_all)


def body(queries, keys, values, tile_mask, out_weight):
    x_hi, z, core, x_lo, y = place()
    q_all, k_all, v_all, m_all, w_all = spread(queries, keys, values, tile_mask, out_weight)
    slots, heads, row_tiles, tiles = m_all.shape
    by_place = m_all.reshape(slots, heads, row_tiles, 2, NZ, 2, row_tiles)
    here = lax.dynamic_index_in_dim(by_place, x_hi, 3, keepdims=False)
    here = lax.dynamic_index_in_dim(here, core, 4, keepdims=False)
    here = here.transpose(1, 3, 4, 0, 2).reshape(heads, NZ * row_tiles, slots * row_tiles)
    bias = jnp.repeat(jnp.where(here > 0, 0.0, BLOCKED).astype(jnp.float32), TILE, axis=2)
    o, stat = attend(bias, q_all, k_all, v_all)
    return merge(o, stat, w_all, queries.shape[0])


def solution(mesh):
    placed = (
        P(("blk", "head"), None),
        P(("blk", "head"), None),
        P(("blk", "head"), None),
        P("head", "blk", None),
        P("head", None),
    )
    return jax.shard_map(
        body, mesh=mesh, in_specs=placed, out_specs=P(("blk", "head"), None), check_vma=False
    )
```

```python
import functools
import math

import jax
import jax.numpy as jnp
from jax import lax
from jax.experimental import pallas as pl
from jax.experimental.pallas import tpu as pltpu
from jax.sharding import PartitionSpec as P

HEAD_DIM = 128
TILE = 128
MESH = pl.DeviceIdType.MESH
TO_LOG2 = math.log2(math.e) / math.sqrt(HEAD_DIM)
LOW = -1e30
BLOCKED = 2e30
VMEM_LIMIT = 60 * 2**20
NX, NY, NZ = 2, 4, 8


def place():
    blk, head = lax.axis_index("blk"), lax.axis_index("head")
    return blk // 16, (blk // 2) % NZ, blk % 2, head // NY, head % NY


def at(x_hi, z, core, x_lo, y):
    return (x_hi * 16 + z * 2 + core, x_lo * NY + y)


def greet(peers):
    barrier = pltpu.get_barrier_semaphore()
    for peer in peers:
        pl.semaphore_signal(barrier, inc=1, device_id=peer, device_id_type=MESH)
    pl.semaphore_wait(barrier, len(peers))


class Wires:
    def __init__(self, send_sems, recv_sems, local_sems):
        self.send_sems, self.recv_sems, self.local_sems = send_sems, recv_sems, local_sems
        self.used, self.used_local = 0, 0
        self.sent = []

    def push(self, src, dst, peer, land=None):
        copy = pltpu.make_async_remote_copy(
            src_ref=src,
            dst_ref=dst,
            send_sem=self.send_sems.at[self.used],
            recv_sem=self.recv_sems.at[self.used],
            device_id=peer,
            device_id_type=MESH,
        )
        arrival = copy
        if land is not None:
            arrival = pltpu.make_async_remote_copy(
                src_ref=land,
                dst_ref=land,
                send_sem=self.send_sems.at[self.used],
                recv_sem=self.recv_sems.at[self.used],
                device_id=peer,
                device_id_type=MESH,
            )
        self.used += 1
        copy.start()
        self.sent.append(copy)
        return arrival

    def local(self, src, dst):
        copy = pltpu.make_async_copy(src, dst, self.local_sems.at[self.used_local])
        self.used_local += 1
        copy.start()
        return copy

    def finish(self):
        for copy in self.sent:
            copy.wait_send()


def fused_kernel(
    q, k, v, m, w,
    out, q_all, k_all, v_all, w_all,
    q_here, k_here, v_here, w_here, m_in, bias, query, acc, top_at, total_at,
    o, stat, o_in, stat_in, ready, mixed_in,
    send_sems, recv_sems, local_sems,
):
    x_hi, z, core, x_lo, y = place()
    rows = q.shape[0]
    heads, q_count = query.shape[0], query.shape[1]
    slots, slab, width = q_here.shape
    row_tiles = slab // TILE
    group = x_lo * NY + y
    other_hi, other_core, other_lo = 1 - x_hi, 1 - core, 1 - x_lo
    slot = x_hi * 2 + core
    sibling = at(x_hi, z, other_core, x_lo, y)
    across = at(other_hi, z, core, x_lo, y)
    diagonal = at(other_hi, z, other_core, x_lo, y)
    z_up, z_down = (z + 1) % NZ, (z + NZ - 1) % NZ
    up, down = at(x_hi, z_up, core, x_lo, y), at(x_hi, z_down, core, x_lo, y)
    y_up, y_down, y_far = (y + 1) % NY, (y + NY - 1) % NY, (y + 2) % NY
    partner = at(x_hi, z, core, other_lo, y)
    outer = at(other_hi, z, core, other_lo, y)
    blk = x_hi * 16 + z * 2 + core
    head_peers = [(group + step) % 8 for step in range(1, 8)]
    greet([(blk, peer) for peer in head_peers] + [sibling, across, diagonal, up, down, outer])
    wires = Wires(send_sems, recv_sems, local_sems)

    def exchange(src, dst):
        arrivals = []
        for step in range(1, 8):
            peer = (group + step) % 8
            origin = (group + 8 - step) % 8
            arrivals.append(
                wires.push(
                    src.at[:, pl.ds(pl.multiple_of(peer * width, 128), width)],
                    dst.at[pl.ds(pl.multiple_of(group * rows, 64), rows), :],
                    (blk, peer),
                    dst.at[pl.ds(pl.multiple_of(origin * rows, 64), rows), :],
                )
            )
        own = wires.local(
            src.at[:, pl.ds(pl.multiple_of(group * width, 128), width)],
            dst.at[pl.ds(pl.multiple_of(group * rows, 64), rows), :],
        )
        return arrivals, own

    def settle(pending):
        for arrival in pending[0]:
            arrival.wait_recv()
        pending[1].wait()

    k_wait = exchange(k, k_all.at[z])
    v_wait = exchange(v, v_all.at[z])
    q_wait = exchange(q, q_all.at[slot])
    m_wait = [
        wires.push(m, m_in.at[slot], sibling, m_in.at[x_hi * 2 + other_core]),
        wires.push(m, m_in.at[slot], across, m_in.at[other_hi * 2 + core]),
        wires.push(m, m_in.at[slot], diagonal, m_in.at[other_hi * 2 + other_core]),
    ]
    m_own = wires.local(m, m_in.at[slot])

    ring, loads = {}, {}

    def ring_step(full, step, direction):
        if direction > 0:
            held = (z + NZ - step) % NZ
            landing = (z + NZ - step - 1) % NZ
            return wires.push(full.at[held], full.at[held], up, full.at[landing]), landing
        held = (z + step) % NZ
        landing = (z + step + 1) % NZ
        return wires.push(full.at[held], full.at[held], down, full.at[landing]), landing

    def load(name, index):
        if name == "k":
            return wires.local(k_all.at[index], k_here.at[index])
        return wires.local(v_all.at[index], v_here.at[index])

    def ring_turn(step):
        loading = []
        for name, full in (("k", k_all), ("v", v_all)):
            for direction in (1, -1):
                key = (name, direction)
                if key not in ring:
                    continue
                arrival, index = ring[key]
                arrival.wait_recv()
                if step < (4 if key in (("k", 1), ("v", -1)) else 3):
                    ring[key] = ring_step(full, step, direction)
                else:
                    del ring[key]
                loading.append(load(name, index))
        return loading

    settle(k_wait)
    ring[("k", 1)] = ring_step(k_all, 0, 1)
    ring[("k", -1)] = ring_step(k_all, 0, -1)
    settle(v_wait)
    ring[("v", 1)] = ring_step(v_all, 0, 1)
    ring[("v", -1)] = ring_step(v_all, 0, -1)
    own_loads = [load("k", z), load("v", z)]

    depth = w.shape[0]
    half = depth // 2
    columns = w.shape[1] // 2
    mine = pl.ds(pl.multiple_of(core * columns, 128), columns)
    theirs = pl.ds(pl.multiple_of(other_core * columns, 128), columns)
    upper, lower, whole = pl.ds(0, half), pl.ds(half, half), pl.ds(0, depth)

    def w_part(lo, yy, part, cols=mine):
        return w_all.at[lo * NY + yy, part, cols]

    def w_cross(source, yy):
        return (
            wires.push(source(upper), w_part(x_lo, yy, upper), partner, w_part(other_lo, yy, upper)),
            wires.push(source(lower), w_part(x_lo, yy, lower), outer, w_part(other_lo, yy, lower)),
        )

    swaps = []

    def w_swap(lo, yy, part):
        swaps.append(
            wires.push(w_part(lo, yy, part), w_part(lo, yy, part), sibling, w_part(lo, yy, part, theirs))
        )

    settle(q_wait)
    q_side = wires.push(q_all.at[slot], q_all.at[slot], sibling, q_all.at[x_hi * 2 + other_core])
    q_across = wires.push(q_all.at[slot], q_all.at[slot], across, q_all.at[other_hi * 2 + core])
    w_up = wires.push(w.at[:, mine], w_part(x_lo, y, whole), (blk, x_lo * NY + y_up), w_part(x_lo, y_down, whole))
    w_down = wires.push(w.at[:, mine], w_part(x_lo, y, whole), (blk, x_lo * NY + y_down), w_part(x_lo, y_up, whole))
    crossing = [w_cross(lambda part: w.at[part, mine], y)]

    acc[...] = jnp.zeros_like(acc)
    stat[...] = jnp.zeros_like(stat)
    top_at[...] = jnp.full_like(top_at, LOW)
    total_at[...] = jnp.zeros_like(total_at)
    for arrival in m_wait:
        arrival.wait_recv()
    m_own.wait()
    tile_rows = slots * row_tiles
    spread_rows = lax.broadcasted_iota(jnp.int32, (tile_rows, q_count), 0)
    spread_cols = lax.broadcasted_iota(jnp.int32, (tile_rows, q_count), 1)
    spread = jnp.where(spread_cols // TILE == spread_rows, 1.0, 0.0).astype(jnp.bfloat16)
    for head in range(heads):
        allowed = jnp.concatenate([m_in[s, head] for s in range(slots)], axis=0)
        allowed = jnp.where(allowed > 0, 1.0, 0.0).astype(jnp.bfloat16)
        wide = lax.dot_general(allowed, spread, (((0,), (0,)), ((), ())), preferred_element_type=jnp.float32)
        bias[head] = (1.0 - wide) * BLOCKED

    q_across.wait_recv()
    q_diagonal = wires.push(
        q_all.at[other_hi * 2 + core],
        q_all.at[other_hi * 2 + core],
        sibling,
        q_all.at[other_hi * 2 + other_core],
    )
    q_side.wait_recv()
    first_turn = ring_turn(1)
    q_diagonal.wait_recv()
    q_load = wires.local(q_all, q_here)
    q_load.wait()
    for head in range(heads):
        for s in range(slots):
            scaled = q_here[s, :, head * HEAD_DIM : (head + 1) * HEAD_DIM].astype(jnp.float32) * TO_LOG2
            coarse = scaled.astype(jnp.bfloat16)
            at_rows = slice(s * slab, (s + 1) * slab)
            query[head, at_rows, :HEAD_DIM] = coarse
            query[head, at_rows, HEAD_DIM:] = (scaled - coarse.astype(jnp.float32)).astype(jnp.bfloat16)

    ones = jnp.ones((16, slab), jnp.bfloat16)

    def work(loading, first, second=None):
        for one in loading:
            one.wait()

        def one_head(i, unused):
            head, turn = i % heads, i // heads
            index = first if second is None else first + turn * (second - first)
            lanes = pl.ds(pl.multiple_of(head * HEAD_DIM, HEAD_DIM), HEAD_DIM)
            key = k_here[index, :, lanes]
            scores = lax.dot_general(
                jnp.concatenate([key, key], axis=1),
                query[head],
                (((1,), (1,)), ((), ())),
                preferred_element_type=jnp.float32,
            )
            first_tile = (x_hi * 2 * NZ + index * 2 + core) * row_tiles
            blocked = [bias[head, pl.ds(first_tile + a, 1), :] for a in range(row_tiles)]
            top = top_at[head]
            next_top = top
            for a in range(row_tiles):
                tile_top = jnp.max(scores[a * TILE : (a + 1) * TILE], axis=0, keepdims=True)
                next_top = jnp.maximum(next_top, tile_top - blocked[a])
            weights = jnp.concatenate(
                [
                    jnp.exp2(scores[a * TILE : (a + 1) * TILE] - (next_top + blocked[a])).astype(jnp.bfloat16)
                    for a in range(row_tiles)
                ],
                axis=0,
            )
            shrink = jnp.exp2(top - next_top)
            added = lax.dot_general(
                jnp.concatenate([v_here[index, :, lanes].T, ones], axis=0),
                weights,
                (((1,), (0,)), ((), ())),
                preferred_element_type=jnp.float32,
            )
            acc[head] = acc[head] * shrink + added[:HEAD_DIM]
            top_at[head] = next_top
            total_at[head] = total_at[head] * shrink + added[HEAD_DIM : HEAD_DIM + 1]
            return unused

        lax.fori_loop(0, heads if second is None else 2 * heads, one_head, 0)

    def crossed(index, yy):
        crossing[index][0].wait_recv()
        w_swap(other_lo, yy, upper)
        crossing[index][1].wait_recv()
        w_swap(other_lo, yy, lower)

    work(own_loads, z)
    work(first_turn, z_down, z_up)
    w_up.wait_recv()
    far_up = wires.push(
        w_part(x_lo, y_down, upper), w_part(x_lo, y_down, upper), (blk, x_lo * NY + y_up), w_part(x_lo, y_far, upper)
    )
    w_down.wait_recv()
    far_down = wires.push(
        w_part(x_lo, y_up, lower), w_part(x_lo, y_up, lower), (blk, x_lo * NY + y_down), w_part(x_lo, y_far, lower)
    )
    crossing.append(w_cross(functools.partial(w_part, x_lo, y_down), y_down))
    crossing.append(w_cross(functools.partial(w_part, x_lo, y_up), y_up))
    w_swap(x_lo, y_down, whole)
    w_swap(x_lo, y_up, whole)
    crossed(0, y)
    turn = ring_turn(2)
    work(turn, (z + NZ - 2) % NZ, (z + 2) % NZ)
    far_up.wait_recv()
    far_down.wait_recv()
    crossing.append(w_cross(functools.partial(w_part, x_lo, y_far), y_far))
    w_swap(x_lo, y_far, whole)
    turn = ring_turn(3)
    crossed(1, y_down)
    crossed(2, y_up)
    work(turn, (z + NZ - 3) % NZ, (z + 3) % NZ)
    turn = ring_turn(4)
    work(turn, (z + 4) % NZ)
    crossed(3, y_far)

    for head in range(heads):
        mean = (acc[head] / jnp.maximum(total_at[head], 1e-30)).astype(jnp.bfloat16)
        for s in range(slots):
            cols = slice(s * slab, (s + 1) * slab)
            o[s, head * HEAD_DIM : (head + 1) * HEAD_DIM, :] = mean[:, cols]
            stat[s, head : head + 1, :] = top_at[head, :, cols]
            stat[s, heads + head : heads + head + 1, :] = total_at[head, :, cols]
    arrivals = []
    for hi, c, peer in ((other_hi, core, across), (other_hi, other_core, diagonal), (x_hi, other_core, sibling)):
        peer_slot = hi * 2 + c
        arrivals.append(wires.push(o.at[peer_slot], o_in.at[slot], peer, o_in.at[peer_slot]))
        arrivals.append(wires.push(stat.at[peer_slot], stat_in.at[slot], peer, stat_in.at[peer_slot]))
    o_in[slot] = o[slot]
    stat_in[slot] = stat[slot]
    for arrival in swaps:
        arrival.wait_recv()
    w_loads = [wires.local(w, w_here.at[group])] + [wires.local(w_all.at[g], w_here.at[g]) for g in head_peers]
    for arrival in arrivals:
        arrival.wait_recv()
    for head in range(heads):
        tops = [stat_in[s, head : head + 1, :] for s in range(slots)]
        best = functools.reduce(jnp.maximum, tops)
        shares = [stat_in[s, heads + head : heads + head + 1, :] * jnp.exp2(tops[s] - best) for s in range(slots)]
        total = functools.reduce(jnp.add, shares)
        band = slice(head * HEAD_DIM, (head + 1) * HEAD_DIM)
        blend = functools.reduce(
            jnp.add,
            [o_in[s, band, :].astype(jnp.float32) * (shares[s] / total) for s in range(slots)],
        )
        ready[:, band] = blend.T.astype(jnp.bfloat16)
    pieces = []
    for step in range(1, 8):
        peer = (group + step) % 8
        origin = (group + 8 - step) % 8
        pieces.append(
            wires.push(
                ready.at[pl.ds(pl.multiple_of(peer * rows, 64), rows), :],
                mixed_in.at[group],
                (blk, peer),
                mixed_in.at[origin],
            )
        )
    mixed_in[group] = ready[pl.ds(pl.multiple_of(group * rows, 64), rows), :]
    for one in w_loads:
        one.wait()
    for piece in pieces:
        piece.wait_recv()
    cols = 768
    for c in range(out.shape[1] // cols):
        mixed = jnp.zeros((rows, cols), jnp.float32)
        for g in range(8):
            mixed += jnp.dot(
                mixed_in[g], w_here[g, :, c * cols : (c + 1) * cols], preferred_element_type=jnp.float32
            )
        out[:, c * cols : (c + 1) * cols] = mixed.astype(jnp.bfloat16)
    wires.finish()


def body(queries, keys, values, tile_mask, out_weight):
    rows = queries.shape[0]
    width = queries.shape[1] // 8
    heads = width // HEAD_DIM
    slab, slots = rows * 8, 4
    q_count = slots * slab
    bf16, f32 = jnp.bfloat16, jnp.float32
    hbm = pl.BlockSpec(memory_space=pl.ANY)
    w_shape = (8,) + out_weight.shape
    return pl.pallas_call(
        fused_kernel,
        out_shape=[
            jax.ShapeDtypeStruct(queries.shape, bf16),
            jax.ShapeDtypeStruct((slots, slab, width), bf16),
            jax.ShapeDtypeStruct((NZ, slab, width), bf16),
            jax.ShapeDtypeStruct((NZ, slab, width), bf16),
            jax.ShapeDtypeStruct(w_shape, bf16),
        ],
        in_specs=[hbm] * 5,
        out_specs=[pl.BlockSpec(memory_space=pltpu.VMEM)] + [hbm] * 4,
        scratch_shapes=[
            pltpu.VMEM((slots, slab, width), bf16),
            pltpu.VMEM((NZ, slab, width), bf16),
            pltpu.VMEM((NZ, slab, width), bf16),
            pltpu.VMEM(w_shape, bf16),
            pltpu.VMEM((slots,) + tile_mask.shape, jnp.int32),
            pltpu.VMEM((heads, tile_mask.shape[2], q_count), f32),
            pltpu.VMEM((heads, q_count, 2 * HEAD_DIM), bf16),
            pltpu.VMEM((heads, HEAD_DIM, q_count), f32),
            pltpu.VMEM((heads, 1, q_count), f32),
            pltpu.VMEM((heads, 1, q_count), f32),
            pltpu.VMEM((slots, width, slab), bf16),
            pltpu.VMEM((slots, 8, slab), f32),
            pltpu.VMEM((slots, width, slab), bf16),
            pltpu.VMEM((slots, 8, slab), f32),
            pltpu.VMEM((slab, width), bf16),
            pltpu.VMEM((8, rows, width), bf16),
            pltpu.SemaphoreType.DMA((80,)),
            pltpu.SemaphoreType.DMA((80,)),
            pltpu.SemaphoreType.DMA((40,)),
        ],
        name="fused",
        compiler_params=pltpu.CompilerParams(
            collective_id=1, has_side_effects=True, vmem_limit_bytes=VMEM_LIMIT
        ),
    )(queries, keys, values, tile_mask, out_weight)[0]


def solution(mesh):
    placed = (
        P(("blk", "head"), None),
        P(("blk", "head"), None),
        P(("blk", "head"), None),
        P("head", "blk", None),
        P("head", None),
    )
    return jax.shard_map(
        body, mesh=mesh, in_specs=placed, out_specs=P(("blk", "head"), None), check_vma=False
    )
```

```python
import functools
import math

import jax
import jax.numpy as jnp
from jax import lax
from jax.experimental import pallas as pl
from jax.experimental.pallas import tpu as pltpu
from jax.sharding import PartitionSpec as P

HEAD_DIM = 128
TILE = 128
MESH = pl.DeviceIdType.MESH
TO_LOG2 = math.log2(math.e) / math.sqrt(HEAD_DIM)
LOW = -1e30
BLOCKED = 2e30
VMEM_LIMIT = 60 * 2**20
NX, NY, NZ = 2, 4, 8


def place():
    blk, head = lax.axis_index("blk"), lax.axis_index("head")
    return blk // 16, (blk // 2) % NZ, blk % 2, head // NY, head % NY


def at(x_hi, z, core, x_lo, y):
    return (x_hi * 16 + z * 2 + core, x_lo * NY + y)


def greet(peers):
    barrier = pltpu.get_barrier_semaphore()
    for peer in peers:
        pl.semaphore_signal(barrier, inc=1, device_id=peer, device_id_type=MESH)
    pl.semaphore_wait(barrier, len(peers))


class Wires:
    def __init__(self, send_sems, recv_sems, local_sems):
        self.send_sems, self.recv_sems, self.local_sems = send_sems, recv_sems, local_sems
        self.used, self.used_local = 0, 0
        self.sent = []

    def push(self, src, dst, peer, land=None):
        copy = pltpu.make_async_remote_copy(
            src_ref=src,
            dst_ref=dst,
            send_sem=self.send_sems.at[self.used],
            recv_sem=self.recv_sems.at[self.used],
            device_id=peer,
            device_id_type=MESH,
        )
        arrival = copy
        if land is not None:
            arrival = pltpu.make_async_remote_copy(
                src_ref=land,
                dst_ref=land,
                send_sem=self.send_sems.at[self.used],
                recv_sem=self.recv_sems.at[self.used],
                device_id=peer,
                device_id_type=MESH,
            )
        self.used += 1
        copy.start()
        self.sent.append(copy)
        return arrival

    def local(self, src, dst):
        copy = pltpu.make_async_copy(src, dst, self.local_sems.at[self.used_local])
        self.used_local += 1
        copy.start()
        return copy

    def finish(self):
        for copy in self.sent:
            copy.wait_send()


def fused_kernel(
    q, k, v, m, w,
    out, k_all, v_all, w_all,
    q_here, k_here, v_here, w_here, m_in, bias, query, acc, top_at, total_at,
    o, stat, o_in, stat_in, ready, mixed_in, mixed, result,
    send_sems, recv_sems, local_sems,
):
    x_hi, z, core, x_lo, y = place()
    rows = q.shape[0]
    heads, slots, slab = q_here.shape[0], q_here.shape[1], q_here.shape[2]
    width = heads * HEAD_DIM
    row_tiles = slab // TILE
    q_count = slots * slab
    group = x_lo * NY + y
    other_hi, other_core, other_lo = 1 - x_hi, 1 - core, 1 - x_lo
    slot = x_hi * 2 + core
    sibling_slot, across_slot, diagonal_slot = x_hi * 2 + other_core, other_hi * 2 + core, other_hi * 2 + other_core
    sibling = at(x_hi, z, other_core, x_lo, y)
    across = at(other_hi, z, core, x_lo, y)
    diagonal = at(other_hi, z, other_core, x_lo, y)
    z_up, z_down = (z + 1) % NZ, (z + NZ - 1) % NZ
    up, down = at(x_hi, z_up, core, x_lo, y), at(x_hi, z_down, core, x_lo, y)
    y_up, y_down, y_far = (y + 1) % NY, (y + NY - 1) % NY, (y + 2) % NY
    partner = at(x_hi, z, core, other_lo, y)
    outer = at(other_hi, z, core, other_lo, y)
    blk = x_hi * 16 + z * 2 + core
    head_peers = [(group + step) % 8 for step in range(1, 8)]
    neighbour = at(x_hi, z, other_core, x_lo, y + 1 - 2 * (y % 2))
    greet([(blk, peer) for peer in head_peers] + [sibling, across, diagonal, up, down, outer, neighbour])
    wires = Wires(send_sems, recv_sems, local_sems)
    my_rows = pl.ds(pl.multiple_of(group * rows, 64), rows)

    def feature(owner, head):
        return pl.ds(pl.multiple_of(owner * width + head * HEAD_DIM, HEAD_DIM), HEAD_DIM)

    def exchange(src, dst, head):
        arrivals = []
        for step in range(1, 8):
            peer = (group + step) % 8
            origin = (group + 8 - step) % 8
            arrivals.append(
                wires.push(
                    src.at[:, feature(peer, head)],
                    dst.at[my_rows, :],
                    (blk, peer),
                    dst.at[pl.ds(pl.multiple_of(origin * rows, 64), rows), :],
                )
            )
        return arrivals, wires.local(src.at[:, feature(group, head)], dst.at[my_rows, :])

    def settle(pending):
        for arrival in pending[0]:
            arrival.wait_recv()
        pending[1].wait()

    waits = {}

    def exchange_head(head):
        waits["k", head] = exchange(k, k_all.at[head, z], head)
        waits["v", head] = exchange(v, v_all.at[head, z], head)
        waits["q", head] = exchange(q, q_here.at[head, slot], head)

    ring = {}

    def ring_step(full, head, step, direction):
        if direction > 0:
            held, landing, peer = (z + NZ - step) % NZ, (z + NZ - step - 1) % NZ, up
        else:
            held, landing, peer = (z + step) % NZ, (z + step + 1) % NZ, down
        here = full.at[head, held]
        return wires.push(here, here, peer, full.at[head, landing]), landing

    def load(name, head, index):
        if name == "k":
            return wires.local(k_all.at[head, index], k_here.at[head, index])
        return wires.local(v_all.at[head, index], v_here.at[head, index])

    def ring_start(head):
        loading = []
        for name, full in (("k", k_all), ("v", v_all)):
            settle(waits[name, head])
            for direction in (1, -1):
                ring[head, name, direction] = ring_step(full, head, 0, direction)
            loading.append(load(name, head, z))
        return loading

    def ring_turn(head, step):
        loading = []
        for name, full in (("k", k_all), ("v", v_all)):
            for direction in (1, -1):
                last = 4 if (name, direction) in (("k", 1), ("v", -1)) else 3
                if step > last:
                    continue
                arrival, index = ring[head, name, direction]
                arrival.wait_recv()
                if step < last:
                    ring[head, name, direction] = ring_step(full, head, step, direction)
                loading.append(load(name, head, index))
        return loading

    moving = {}

    def queries_out(head):
        settle(waits["q", head])
        mine = q_here.at[head, slot]
        moving["side", head] = wires.push(mine, mine, sibling, q_here.at[head, sibling_slot])
        moving["across", head] = wires.push(mine, mine, across, q_here.at[head, across_slot])

    def queries_on(head):
        moving["across", head].wait_recv()
        theirs = q_here.at[head, across_slot]
        moving["diagonal", head] = wires.push(theirs, theirs, sibling, q_here.at[head, diagonal_slot])

    def queries_in(head):
        moving["side", head].wait_recv()
        moving["diagonal", head].wait_recv()
        for s in range(slots):
            scaled = q_here[head, s].astype(jnp.float32) * TO_LOG2
            coarse = scaled.astype(jnp.bfloat16)
            at_rows = slice(s * slab, (s + 1) * slab)
            query[head, at_rows, :HEAD_DIM] = coarse
            query[head, at_rows, HEAD_DIM:] = (scaled - coarse.astype(jnp.float32)).astype(jnp.bfloat16)

    depth = w.shape[0]
    half = depth // 2
    quarter = w.shape[1] // 4
    parity = y % 2
    y_pair = y + 1 - 2 * parity
    beside = at(x_hi, z, core, x_lo, y_pair)
    mine = pl.ds(pl.multiple_of((parity * 2 + core) * quarter, 128), quarter)
    next_door = pl.ds(pl.multiple_of(((1 - parity) * 2 + core) * quarter, 128), quarter)
    upper, lower = pl.ds(0, half), pl.ds(half, half)

    def w_along(peer_y, from_y, cols):
        return wires.push(w.at[:, cols], w_all.at[group], (blk, x_lo * NY + peer_y), w_all.at[x_lo * NY + from_y])

    def w_cross(yy, own=False):
        arrivals = []
        for part, peer in ((upper, partner), (lower, outer)):
            held = w.at[part, mine] if own else w_all.at[x_lo * NY + yy, part]
            arrivals.append(
                wires.push(held, w_all.at[x_lo * NY + yy, part], peer, w_all.at[other_lo * NY + yy, part])
            )
        return arrivals

    def make_bias(head):
        tile_rows = slots * row_tiles
        spread_rows = lax.broadcasted_iota(jnp.int32, (tile_rows, q_count), 0)
        spread_cols = lax.broadcasted_iota(jnp.int32, (tile_rows, q_count), 1)
        spread = jnp.where(spread_cols // TILE == spread_rows, 1.0, 0.0).astype(jnp.bfloat16)
        allowed = jnp.concatenate([m_in[s, head] for s in range(slots)], axis=0)
        allowed = jnp.where(allowed > 0, 1.0, 0.0).astype(jnp.bfloat16)
        wide = lax.dot_general(allowed, spread, (((0,), (0,)), ((), ())), preferred_element_type=jnp.float32)
        bias[head] = (1.0 - wide) * BLOCKED

    ones = jnp.ones((16, slab), jnp.bfloat16)

    def work(head, loading, first, second=None):
        for one in loading:
            one.wait()

        def one_block(i, unused):
            index = first if second is None else first + i * (second - first)
            key = k_here[head, index]
            scores = lax.dot_general(
                jnp.concatenate([key, key], axis=1),
                query[head],
                (((1,), (1,)), ((), ())),
                preferred_element_type=jnp.float32,
            )
            first_tile = (x_hi * 2 * NZ + index * 2 + core) * row_tiles
            blocked = [bias[head, pl.ds(first_tile + a, 1), :] for a in range(row_tiles)]
            top = top_at[head]
            next_top = top
            for a in range(row_tiles):
                tile_top = jnp.max(scores[a * TILE : (a + 1) * TILE], axis=0, keepdims=True)
                next_top = jnp.maximum(next_top, tile_top - blocked[a])
            weights = jnp.concatenate(
                [
                    jnp.exp2(scores[a * TILE : (a + 1) * TILE] - (next_top + blocked[a])).astype(jnp.bfloat16)
                    for a in range(row_tiles)
                ],
                axis=0,
            )
            shrink = jnp.exp2(top - next_top)
            added = lax.dot_general(
                jnp.concatenate([v_here[head, index].T, ones], axis=0),
                weights,
                (((1,), (0,)), ((), ())),
                preferred_element_type=jnp.float32,
            )
            acc[head] = acc[head] * shrink + added[:HEAD_DIM]
            top_at[head] = next_top
            total_at[head] = total_at[head] * shrink + added[HEAD_DIM : HEAD_DIM + 1]
            return unused

        lax.fori_loop(0, 1 if second is None else 2, one_block, 0)

    def partial_out(head):
        mean = (acc[head] / jnp.maximum(total_at[head], 1e-30)).astype(jnp.bfloat16)
        for s in range(slots):
            cols = slice(s * slab, (s + 1) * slab)
            o[head, s] = mean[:, cols]
            stat[head, s, 0:1, :] = top_at[head, :, cols]
            stat[head, s, 1:2, :] = total_at[head, :, cols]
        arrivals = []
        for peer_slot, peer in ((across_slot, across), (diagonal_slot, diagonal), (sibling_slot, sibling)):
            arrivals.append(wires.push(o.at[head, peer_slot], o_in.at[head, slot], peer, o_in.at[head, peer_slot]))
            arrivals.append(
                wires.push(stat.at[head, peer_slot], stat_in.at[head, slot], peer, stat_in.at[head, peer_slot])
            )
        o_in[head, slot] = o[head, slot]
        stat_in[head, slot] = stat[head, slot]
        return arrivals

    def partial_in(head, arrivals):
        for arrival in arrivals:
            arrival.wait_recv()
        tops = [stat_in[head, s, 0:1, :] for s in range(slots)]
        best = functools.reduce(jnp.maximum, tops)
        shares = [stat_in[head, s, 1:2, :] * jnp.exp2(tops[s] - best) for s in range(slots)]
        total = functools.reduce(jnp.add, shares)
        blend = functools.reduce(
            jnp.add, [o_in[head, s].astype(jnp.float32) * (shares[s] / total) for s in range(slots)]
        )
        ready[head] = blend.T.astype(jnp.bfloat16)
        my_lanes = pl.ds(pl.multiple_of(group * HEAD_DIM, HEAD_DIM), HEAD_DIM)
        pieces = []
        for step in range(1, 8):
            peer = (group + step) % 8
            origin = (group + 8 - step) % 8
            pieces.append(
                wires.push(
                    ready.at[head, pl.ds(pl.multiple_of(peer // 2 * 2 * rows, 128), 2 * rows), :],
                    mixed_in.at[head, core, :, my_lanes],
                    (blk, peer),
                    mixed_in.at[head, core, :, pl.ds(pl.multiple_of(origin * HEAD_DIM, HEAD_DIM), HEAD_DIM)],
                )
            )
        mixed_in[head, core, :, my_lanes] = ready[head, pl.ds(pl.multiple_of(group // 2 * 2 * rows, 128), 2 * rows), :]
        return pieces

    def share(head, pieces):
        for piece in pieces:
            piece.wait_recv()
        held = mixed_in.at[head, core]
        return wires.push(held, held, sibling, mixed_in.at[head, other_core])

    def project(head, shared):
        shared.wait_recv()
        tokens = mixed_in[head].reshape(4 * rows, 8 * HEAD_DIM)
        part = jnp.dot(tokens, w_here[head], preferred_element_type=jnp.float32)
        if head == 0:
            mixed[...] = part
        elif head < heads - 1:
            mixed[...] += part
        else:
            result[...] = (mixed[...] + part).astype(jnp.bfloat16)

    def pair(step):
        return (z + NZ - step) % NZ, (z + step) % NZ

    exchange_head(0)
    m_wait = [
        wires.push(m, m_in.at[slot], sibling, m_in.at[sibling_slot]),
        wires.push(m, m_in.at[slot], across, m_in.at[across_slot]),
        wires.push(m, m_in.at[slot], diagonal, m_in.at[diagonal_slot]),
    ]
    m_own = wires.local(m, m_in.at[slot])
    exchange_head(1)
    own = [ring_start(0)]
    queries_out(0)
    exchange_head(2)
    own.append(ring_start(1))
    queries_out(1)
    own.append(ring_start(2))
    queries_out(2)
    w_crossed = [w_cross(y, True)]
    w_near = [w_along(y_up, y_down, next_door), w_along(y_down, y_up, next_door)]
    w_far = w_along(y_far, y_far, mine)
    acc[...] = jnp.zeros_like(acc)
    stat[...] = jnp.zeros_like(stat)
    top_at[...] = jnp.full_like(top_at, LOW)
    total_at[...] = jnp.zeros_like(total_at)
    for arrival in m_wait:
        arrival.wait_recv()
    m_own.wait()
    for head in range(heads):
        make_bias(head)

    for head in range(heads):
        queries_on(head)
        turn = ring_turn(head, 1)
        queries_in(head)
        work(head, own[head], z)
        work(head, turn, *pair(1))
    for head in range(heads):
        work(head, ring_turn(head, 2), *pair(2))
    for arrival in w_near:
        arrival.wait_recv()
    w_crossed += [w_cross(y_down), w_cross(y_up)]
    w_far.wait_recv()
    w_crossed.append(w_cross(y_far))
    for head in range(heads):
        work(head, ring_turn(head, 3), *pair(3))
    partial = []
    for head in range(heads - 1):
        work(head, ring_turn(head, 4), (z + 4) % NZ)
        partial.append(partial_out(head))
    turn = ring_turn(heads - 1, 4)
    for arrivals in w_crossed:
        for arrival in arrivals:
            arrival.wait_recv()
    w_loads = []
    for head in range(heads):
        band = pl.ds(head * HEAD_DIM, HEAD_DIM)
        for owner, source in [(group, w.at[:, mine])] + [(g, w_all.at[g]) for g in head_peers]:
            to_band = pl.ds(pl.multiple_of(owner * HEAD_DIM, HEAD_DIM), HEAD_DIM)
            w_loads.append(wires.local(source.at[band, :], w_here.at[head, to_band, :]))
    pieces = [partial_in(0, partial[0])]
    work(heads - 1, turn, (z + 4) % NZ)
    partial.append(partial_out(heads - 1))
    pieces.append(partial_in(1, partial[1]))
    shared = [share(0, pieces[0])]
    pieces.append(partial_in(2, partial[2]))
    shared.append(share(1, pieces[1]))
    for one in w_loads:
        one.wait()
    project(0, shared[0])
    project(1, shared[1])
    shared.append(share(2, pieces[2]))
    project(2, shared[2])

    def result_rows(c, odd):
        return pl.ds(pl.multiple_of((c * 2 + odd) * rows, 64), rows)

    from_core = pl.ds(pl.multiple_of((parity * 2 + other_core) * quarter, 128), quarter)
    from_beside = pl.ds(pl.multiple_of(((1 - parity) * 2 + core) * quarter, 128), quarter)
    from_opposite = pl.ds(pl.multiple_of(((1 - parity) * 2 + other_core) * quarter, 128), quarter)
    returns = [
        wires.push(result.at[result_rows(core, 1 - parity), :], out.at[:, mine], beside, out.at[:, from_beside]),
        wires.push(result.at[result_rows(other_core, 1 - parity), :], out.at[:, mine], neighbour, out.at[:, from_opposite]),
        wires.push(result.at[result_rows(other_core, parity), :], out.at[:, mine], sibling, out.at[:, from_core]),
    ]
    out[:, mine] = result[result_rows(core, parity), :]
    for arrival in returns:
        arrival.wait_recv()
    wires.finish()


def body(queries, keys, values, tile_mask, out_weight):
    rows, features = queries.shape
    heads = tile_mask.shape[0]
    slab, slots = rows * 8, 4
    q_count = slots * slab
    bf16, f32 = jnp.bfloat16, jnp.float32
    hbm = pl.BlockSpec(memory_space=pl.ANY)
    quarter = out_weight.shape[1] // 4
    w_shape = (8, out_weight.shape[0], quarter)
    vmem = pltpu.VMEM
    return pl.pallas_call(
        fused_kernel,
        out_shape=[
            jax.ShapeDtypeStruct(queries.shape, bf16),
            jax.ShapeDtypeStruct((heads, NZ, slab, HEAD_DIM), bf16),
            jax.ShapeDtypeStruct((heads, NZ, slab, HEAD_DIM), bf16),
            jax.ShapeDtypeStruct(w_shape, bf16),
        ],
        in_specs=[hbm] * 5,
        out_specs=[pl.BlockSpec(memory_space=vmem)] + [hbm] * 3,
        scratch_shapes=[
            vmem((heads, slots, slab, HEAD_DIM), bf16),
            vmem((heads, NZ, slab, HEAD_DIM), bf16),
            vmem((heads, NZ, slab, HEAD_DIM), bf16),
            vmem((heads, 8 * HEAD_DIM, quarter), bf16),
            vmem((slots,) + tile_mask.shape, jnp.int32),
            vmem((heads, tile_mask.shape[2], q_count), f32),
            vmem((heads, q_count, 2 * HEAD_DIM), bf16),
            vmem((heads, HEAD_DIM, q_count), f32),
            vmem((heads, 1, q_count), f32),
            vmem((heads, 1, q_count), f32),
            vmem((heads, slots, HEAD_DIM, slab), bf16),
            vmem((heads, slots, 8, slab), f32),
            vmem((heads, slots, HEAD_DIM, slab), bf16),
            vmem((heads, slots, 8, slab), f32),
            vmem((heads, slab, HEAD_DIM), bf16),
            vmem((heads, 2, 2 * rows, 8 * HEAD_DIM), bf16),
            vmem((4 * rows, quarter), f32),
            vmem((4 * rows, quarter), bf16),
            pltpu.SemaphoreType.DMA((192,)),
            pltpu.SemaphoreType.DMA((192,)),
            pltpu.SemaphoreType.DMA((96,)),
        ],
        name="fused",
        compiler_params=pltpu.CompilerParams(
            collective_id=1, has_side_effects=True, vmem_limit_bytes=VMEM_LIMIT
        ),
    )(queries, keys, values, tile_mask, out_weight)[0]


def solution(mesh):
    placed = (
        P(("blk", "head"), None),
        P(("blk", "head"), None),
        P(("blk", "head"), None),
        P("head", "blk", None),
        P("head", None),
    )
    return jax.shard_map(
        body, mesh=mesh, in_specs=placed, out_specs=P(("blk", "head"), None), check_vma=False
    )
```

```python
import functools
import math

import jax
import jax.numpy as jnp
from jax import lax
from jax.experimental import pallas as pl
from jax.experimental.pallas import tpu as pltpu
from jax.sharding import PartitionSpec as P

HEAD_DIM = 128
TILE = 128
MESH = pl.DeviceIdType.MESH
TO_LOG2 = math.log2(math.e) / math.sqrt(HEAD_DIM)
LOW = -1e30
BLOCKED = 2e30
VMEM_LIMIT = 60 * 2**20
NX, NY, NZ = 2, 4, 8


def place():
    blk, head = lax.axis_index("blk"), lax.axis_index("head")
    return blk // 16, (blk // 2) % NZ, blk % 2, head // NY, head % NY


def at(x_hi, z, core, x_lo, y):
    return (x_hi * 16 + z * 2 + core, x_lo * NY + y)


def greet(peers):
    barrier = pltpu.get_barrier_semaphore()
    for peer in peers:
        pl.semaphore_signal(barrier, inc=1, device_id=peer, device_id_type=MESH)
    pl.semaphore_wait(barrier, len(peers))


class Wires:
    def __init__(self, send_sems, recv_sems, local_sems):
        self.send_sems, self.recv_sems, self.local_sems = send_sems, recv_sems, local_sems
        self.used, self.used_local = 0, 0
        self.sent = []

    def push(self, src, dst, peer, land=None):
        copy = pltpu.make_async_remote_copy(
            src_ref=src,
            dst_ref=dst,
            send_sem=self.send_sems.at[self.used],
            recv_sem=self.recv_sems.at[self.used],
            device_id=peer,
            device_id_type=MESH,
        )
        arrival = copy
        if land is not None:
            arrival = pltpu.make_async_remote_copy(
                src_ref=land,
                dst_ref=land,
                send_sem=self.send_sems.at[self.used],
                recv_sem=self.recv_sems.at[self.used],
                device_id=peer,
                device_id_type=MESH,
            )
        self.used += 1
        copy.start()
        self.sent.append(copy)
        return arrival

    def local(self, src, dst):
        copy = pltpu.make_async_copy(src, dst, self.local_sems.at[self.used_local])
        self.used_local += 1
        copy.start()
        return copy

    def finish(self):
        for copy in self.sent:
            copy.wait_send()


def fused_kernel(
    q, k, v, m, w,
    out, k_all, v_all, w_all,
    q_here, k_here, v_here, w_here, m_in, bias, query, acc, top_at, total_at,
    o, stat, o_in, stat_in, o_chip, stat_chip, o_far, stat_far, ready, mixed_in, mixed, result,
    send_sems, recv_sems, local_sems,
):
    x_hi, z, core, x_lo, y = place()
    rows = q.shape[0]
    heads, slots, slab = q_here.shape[0], q_here.shape[1], q_here.shape[2]
    width = heads * HEAD_DIM
    row_tiles = slab // TILE
    q_count = slots * slab
    group = x_lo * NY + y
    other_hi, other_core, other_lo = 1 - x_hi, 1 - core, 1 - x_lo
    slot = x_hi * 2 + core
    sibling_slot, across_slot, diagonal_slot = x_hi * 2 + other_core, other_hi * 2 + core, other_hi * 2 + other_core
    sibling = at(x_hi, z, other_core, x_lo, y)
    across = at(other_hi, z, core, x_lo, y)
    diagonal = at(other_hi, z, other_core, x_lo, y)
    z_up, z_down = (z + 1) % NZ, (z + NZ - 1) % NZ
    up, down = at(x_hi, z_up, core, x_lo, y), at(x_hi, z_down, core, x_lo, y)
    y_up, y_down, y_far = (y + 1) % NY, (y + NY - 1) % NY, (y + 2) % NY
    partner = at(x_hi, z, core, other_lo, y)
    outer = at(other_hi, z, core, other_lo, y)
    blk = x_hi * 16 + z * 2 + core
    head_peers = [(group + step) % 8 for step in range(1, 8)]
    neighbour = at(x_hi, z, other_core, x_lo, y + 1 - 2 * (y % 2))
    greet([(blk, peer) for peer in head_peers] + [sibling, across, diagonal, up, down, outer, neighbour])
    wires = Wires(send_sems, recv_sems, local_sems)
    my_rows = pl.ds(pl.multiple_of(group * rows, 64), rows)

    def feature(owner, head):
        return pl.ds(pl.multiple_of(owner * width + head * HEAD_DIM, HEAD_DIM), HEAD_DIM)

    def exchange(src, dst, head):
        arrivals = []
        for step in range(1, 8):
            peer = (group + step) % 8
            origin = (group + 8 - step) % 8
            arrivals.append(
                wires.push(
                    src.at[:, feature(peer, head)],
                    dst.at[my_rows, :],
                    (blk, peer),
                    dst.at[pl.ds(pl.multiple_of(origin * rows, 64), rows), :],
                )
            )
        return arrivals, wires.local(src.at[:, feature(group, head)], dst.at[my_rows, :])

    def settle(pending):
        for arrival in pending[0]:
            arrival.wait_recv()
        pending[1].wait()

    waits = {}

    def exchange_head(head):
        waits["k", head] = exchange(k, k_all.at[head, z], head)
        waits["v", head] = exchange(v, v_all.at[head, z], head)
        waits["q", head] = exchange(q, q_here.at[head, slot], head)

    ring = {}

    def ring_step(full, head, step, direction):
        if direction > 0:
            held, landing, peer = (z + NZ - step) % NZ, (z + NZ - step - 1) % NZ, up
        else:
            held, landing, peer = (z + step) % NZ, (z + step + 1) % NZ, down
        here = full.at[head, held]
        return wires.push(here, here, peer, full.at[head, landing]), landing

    def load(name, head, index):
        if name == "k":
            return wires.local(k_all.at[head, index], k_here.at[head, index])
        return wires.local(v_all.at[head, index], v_here.at[head, index])

    def ring_start(head):
        loading = []
        for name, full in (("k", k_all), ("v", v_all)):
            settle(waits[name, head])
            for direction in (1, -1):
                ring[head, name, direction] = ring_step(full, head, 0, direction)
            loading.append(load(name, head, z))
        return loading

    def ring_turn(head, step):
        loading = []
        for name, full in (("k", k_all), ("v", v_all)):
            for direction in (1, -1):
                last = 4 if (name, direction) in (("k", 1), ("v", -1)) else 3
                if step > last:
                    continue
                arrival, index = ring[head, name, direction]
                arrival.wait_recv()
                if step < last:
                    ring[head, name, direction] = ring_step(full, head, step, direction)
                loading.append(load(name, head, index))
        return loading

    moving = {}

    def queries_out(head):
        settle(waits["q", head])
        mine = q_here.at[head, slot]
        moving["side", head] = wires.push(mine, mine, sibling, q_here.at[head, sibling_slot])
        moving["across", head] = wires.push(mine, mine, across, q_here.at[head, across_slot])

    def queries_on(head):
        moving["across", head].wait_recv()
        theirs = q_here.at[head, across_slot]
        moving["diagonal", head] = wires.push(theirs, theirs, sibling, q_here.at[head, diagonal_slot])

    def queries_in(head):
        moving["side", head].wait_recv()
        moving["diagonal", head].wait_recv()
        for s in range(slots):
            scaled = q_here[head, s].astype(jnp.float32) * TO_LOG2
            coarse = scaled.astype(jnp.bfloat16)
            at_rows = slice(s * slab, (s + 1) * slab)
            query[head, at_rows, :HEAD_DIM] = coarse
            query[head, at_rows, HEAD_DIM:] = (scaled - coarse.astype(jnp.float32)).astype(jnp.bfloat16)

    depth = w.shape[0]
    half = depth // 2
    quarter = w.shape[1] // 4
    parity = y % 2
    y_pair = y + 1 - 2 * parity
    beside = at(x_hi, z, core, x_lo, y_pair)
    mine = pl.ds(pl.multiple_of((parity * 2 + core) * quarter, 128), quarter)
    next_door = pl.ds(pl.multiple_of(((1 - parity) * 2 + core) * quarter, 128), quarter)
    upper, lower = pl.ds(0, half), pl.ds(half, half)

    def w_along(peer_y, from_y, cols):
        return wires.push(w.at[:, cols], w_all.at[group], (blk, x_lo * NY + peer_y), w_all.at[x_lo * NY + from_y])

    def w_cross(yy, own=False):
        arrivals = []
        for part, peer in ((upper, partner), (lower, outer)):
            held = w.at[part, mine] if own else w_all.at[x_lo * NY + yy, part]
            arrivals.append(
                wires.push(held, w_all.at[x_lo * NY + yy, part], peer, w_all.at[other_lo * NY + yy, part])
            )
        return arrivals

    def make_bias(head):
        tile_rows = slots * row_tiles
        spread_rows = lax.broadcasted_iota(jnp.int32, (tile_rows, q_count), 0)
        spread_cols = lax.broadcasted_iota(jnp.int32, (tile_rows, q_count), 1)
        spread = jnp.where(spread_cols // TILE == spread_rows, 1.0, 0.0).astype(jnp.bfloat16)
        allowed = jnp.concatenate([m_in[s, head] for s in range(slots)], axis=0)
        allowed = jnp.where(allowed > 0, 1.0, 0.0).astype(jnp.bfloat16)
        wide = lax.dot_general(allowed, spread, (((0,), (0,)), ((), ())), preferred_element_type=jnp.float32)
        bias[head] = (1.0 - wide) * BLOCKED

    ones = jnp.ones((16, slab), jnp.bfloat16)

    def work(head, loading, first, second=None):
        for one in loading:
            one.wait()

        def one_block(i, unused):
            index = first if second is None else first + i * (second - first)
            key = k_here[head, index]
            scores = lax.dot_general(
                jnp.concatenate([key, key], axis=1),
                query[head],
                (((1,), (1,)), ((), ())),
                preferred_element_type=jnp.float32,
            )
            first_tile = (x_hi * 2 * NZ + index * 2 + core) * row_tiles
            blocked = [bias[head, pl.ds(first_tile + a, 1), :] for a in range(row_tiles)]
            top = top_at[head]
            next_top = top
            for a in range(row_tiles):
                tile_top = jnp.max(scores[a * TILE : (a + 1) * TILE], axis=0, keepdims=True)
                next_top = jnp.maximum(next_top, tile_top - blocked[a])
            weights = jnp.concatenate(
                [
                    jnp.exp2(scores[a * TILE : (a + 1) * TILE] - (next_top + blocked[a])).astype(jnp.bfloat16)
                    for a in range(row_tiles)
                ],
                axis=0,
            )
            shrink = jnp.exp2(top - next_top)
            added = lax.dot_general(
                jnp.concatenate([v_here[head, index].T, ones], axis=0),
                weights,
                (((1,), (0,)), ((), ())),
                preferred_element_type=jnp.float32,
            )
            acc[head] = acc[head] * shrink + added[:HEAD_DIM]
            top_at[head] = next_top
            total_at[head] = total_at[head] * shrink + added[HEAD_DIM : HEAD_DIM + 1]
            return unused

        lax.fori_loop(0, 1 if second is None else 2, one_block, 0)

    def blended(parts):
        best = functools.reduce(jnp.maximum, [st[0:1, :] for _, st in parts])
        shares = [st[1:2, :] * jnp.exp2(st[0:1, :] - best) for _, st in parts]
        total = functools.reduce(jnp.add, shares)
        safe = jnp.maximum(total, 1e-30)
        mean = functools.reduce(
            jnp.add, [part.astype(jnp.float32) * (one / safe) for (part, _), one in zip(parts, shares)]
        )
        return mean, best, total

    def partial_out(head):
        mean = (acc[head] / jnp.maximum(total_at[head], 1e-30)).astype(jnp.bfloat16)
        for s in range(slots):
            cols = slice(s * slab, (s + 1) * slab)
            o[head, s % 2, s // 2] = mean[:, cols]
            stat[head, s % 2, s // 2, 0:1, :] = top_at[head, :, cols]
            stat[head, s % 2, s // 2, 1:2, :] = total_at[head, :, cols]
        return [
            wires.push(o.at[head, other_core], o_in.at[head], sibling, o_in.at[head]),
            wires.push(stat.at[head, other_core], stat_in.at[head], sibling, stat_in.at[head]),
        ]

    def partial_on(head, arrivals):
        for arrival in arrivals:
            arrival.wait_recv()
        for hi in range(2):
            mean, best, total = blended(
                [(o[head, core, hi], stat[head, core, hi]), (o_in[head, hi], stat_in[head, hi])]
            )
            o_chip[head, hi] = mean.astype(jnp.bfloat16)
            stat_chip[head, hi, 0:1, :] = best
            stat_chip[head, hi, 1:2, :] = total
        return [
            wires.push(o_chip.at[head, other_hi], o_far.at[head], across, o_far.at[head]),
            wires.push(stat_chip.at[head, other_hi], stat_far.at[head], across, stat_far.at[head]),
        ]

    def partial_in(head, arrivals):
        for arrival in arrivals:
            arrival.wait_recv()
        mean, _, _ = blended([(o_chip[head, x_hi], stat_chip[head, x_hi]), (o_far[head], stat_far[head])])
        ready[head] = mean.T.astype(jnp.bfloat16)
        my_lanes = pl.ds(pl.multiple_of(group * HEAD_DIM, HEAD_DIM), HEAD_DIM)
        pieces = []
        for step in range(1, 8):
            peer = (group + step) % 8
            origin = (group + 8 - step) % 8
            pieces.append(
                wires.push(
                    ready.at[head, pl.ds(pl.multiple_of(peer // 2 * 2 * rows, 128), 2 * rows), :],
                    mixed_in.at[head, core, :, my_lanes],
                    (blk, peer),
                    mixed_in.at[head, core, :, pl.ds(pl.multiple_of(origin * HEAD_DIM, HEAD_DIM), HEAD_DIM)],
                )
            )
        mixed_in[head, core, :, my_lanes] = ready[head, pl.ds(pl.multiple_of(group // 2 * 2 * rows, 128), 2 * rows), :]
        return pieces

    def share(head, pieces):
        for piece in pieces:
            piece.wait_recv()
        held = mixed_in.at[head, core]
        return wires.push(held, held, sibling, mixed_in.at[head, other_core])

    def project(head, shared):
        shared.wait_recv()
        tokens = mixed_in[head].reshape(4 * rows, 8 * HEAD_DIM)
        part = jnp.dot(tokens, w_here[head], preferred_element_type=jnp.float32)
        if head == 0:
            mixed[...] = part
        elif head < heads - 1:
            mixed[...] += part
        else:
            result[...] = (mixed[...] + part).astype(jnp.bfloat16)

    def pair(step):
        return (z + NZ - step) % NZ, (z + step) % NZ

    exchange_head(0)
    m_wait = [
        wires.push(m, m_in.at[slot], sibling, m_in.at[sibling_slot]),
        wires.push(m, m_in.at[slot], across, m_in.at[across_slot]),
        wires.push(m, m_in.at[slot], diagonal, m_in.at[diagonal_slot]),
    ]
    m_own = wires.local(m, m_in.at[slot])
    exchange_head(1)
    own = [ring_start(0)]
    queries_out(0)
    exchange_head(2)
    own.append(ring_start(1))
    queries_out(1)
    own.append(ring_start(2))
    queries_out(2)
    w_crossed = [w_cross(y, True)]
    w_near = [w_along(y_up, y_down, next_door), w_along(y_down, y_up, next_door)]
    w_far = w_along(y_far, y_far, mine)
    acc[...] = jnp.zeros_like(acc)
    stat[...] = jnp.zeros_like(stat)
    stat_chip[...] = jnp.zeros_like(stat_chip)
    top_at[...] = jnp.full_like(top_at, LOW)
    total_at[...] = jnp.zeros_like(total_at)
    for arrival in m_wait:
        arrival.wait_recv()
    m_own.wait()
    for head in range(heads):
        make_bias(head)

    for head in range(heads):
        queries_on(head)
        turn = ring_turn(head, 1)
        queries_in(head)
        work(head, own[head], z)
        work(head, turn, *pair(1))
    for head in range(heads):
        work(head, ring_turn(head, 2), *pair(2))
    for arrival in w_near:
        arrival.wait_recv()
    w_crossed += [w_cross(y_down), w_cross(y_up)]
    w_far.wait_recv()
    w_crossed.append(w_cross(y_far))
    for head in range(heads):
        work(head, ring_turn(head, 3), *pair(3))
    partial = []
    for head in range(heads - 1):
        work(head, ring_turn(head, 4), (z + 4) % NZ)
        partial.append(partial_out(head))
    turn = ring_turn(heads - 1, 4)
    partial[0] = partial_on(0, partial[0])
    work(heads - 1, turn, (z + 4) % NZ)
    partial.append(partial_out(heads - 1))
    partial[1] = partial_on(1, partial[1])
    pieces = [partial_in(0, partial[0])]
    partial[2] = partial_on(2, partial[2])
    for arrivals in w_crossed:
        for arrival in arrivals:
            arrival.wait_recv()
    w_loads = []
    for head in range(heads):
        band = pl.ds(head * HEAD_DIM, HEAD_DIM)
        for owner, source in [(group, w.at[:, mine])] + [(g, w_all.at[g]) for g in head_peers]:
            to_band = pl.ds(pl.multiple_of(owner * HEAD_DIM, HEAD_DIM), HEAD_DIM)
            w_loads.append(wires.local(source.at[band, :], w_here.at[head, to_band, :]))
    pieces.append(partial_in(1, partial[1]))
    shared = [share(0, pieces[0])]
    pieces.append(partial_in(2, partial[2]))
    shared.append(share(1, pieces[1]))
    for one in w_loads:
        one.wait()
    project(0, shared[0])
    project(1, shared[1])
    shared.append(share(2, pieces[2]))
    project(2, shared[2])

    def result_rows(c, odd):
        return pl.ds(pl.multiple_of((c * 2 + odd) * rows, 64), rows)

    from_core = pl.ds(pl.multiple_of((parity * 2 + other_core) * quarter, 128), quarter)
    from_beside = pl.ds(pl.multiple_of(((1 - parity) * 2 + core) * quarter, 128), quarter)
    from_opposite = pl.ds(pl.multiple_of(((1 - parity) * 2 + other_core) * quarter, 128), quarter)
    returns = [
        wires.push(result.at[result_rows(core, 1 - parity), :], out.at[:, mine], beside, out.at[:, from_beside]),
        wires.push(result.at[result_rows(other_core, 1 - parity), :], out.at[:, mine], neighbour, out.at[:, from_opposite]),
        wires.push(result.at[result_rows(other_core, parity), :], out.at[:, mine], sibling, out.at[:, from_core]),
    ]
    out[:, mine] = result[result_rows(core, parity), :]
    for arrival in returns:
        arrival.wait_recv()
    wires.finish()


def body(queries, keys, values, tile_mask, out_weight):
    rows, features = queries.shape
    heads = tile_mask.shape[0]
    slab, slots = rows * 8, 4
    q_count = slots * slab
    bf16, f32 = jnp.bfloat16, jnp.float32
    hbm = pl.BlockSpec(memory_space=pl.ANY)
    quarter = out_weight.shape[1] // 4
    w_shape = (8, out_weight.shape[0], quarter)
    vmem = pltpu.VMEM
    return pl.pallas_call(
        fused_kernel,
        out_shape=[
            jax.ShapeDtypeStruct(queries.shape, bf16),
            jax.ShapeDtypeStruct((heads, NZ, slab, HEAD_DIM), bf16),
            jax.ShapeDtypeStruct((heads, NZ, slab, HEAD_DIM), bf16),
            jax.ShapeDtypeStruct(w_shape, bf16),
        ],
        in_specs=[hbm] * 5,
        out_specs=[pl.BlockSpec(memory_space=vmem)] + [hbm] * 3,
        scratch_shapes=[
            vmem((heads, slots, slab, HEAD_DIM), bf16),
            vmem((heads, NZ, slab, HEAD_DIM), bf16),
            vmem((heads, NZ, slab, HEAD_DIM), bf16),
            vmem((heads, 8 * HEAD_DIM, quarter), bf16),
            vmem((slots,) + tile_mask.shape, jnp.int32),
            vmem((heads, tile_mask.shape[2], q_count), f32),
            vmem((heads, q_count, 2 * HEAD_DIM), bf16),
            vmem((heads, HEAD_DIM, q_count), f32),
            vmem((heads, 1, q_count), f32),
            vmem((heads, 1, q_count), f32),
            vmem((heads, 2, 2, HEAD_DIM, slab), bf16),
            vmem((heads, 2, 2, 8, slab), f32),
            vmem((heads, 2, HEAD_DIM, slab), bf16),
            vmem((heads, 2, 8, slab), f32),
            vmem((heads, 2, HEAD_DIM, slab), bf16),
            vmem((heads, 2, 8, slab), f32),
            vmem((heads, HEAD_DIM, slab), bf16),
            vmem((heads, 8, slab), f32),
            vmem((heads, slab, HEAD_DIM), bf16),
            vmem((heads, 2, 2 * rows, 8 * HEAD_DIM), bf16),
            vmem((4 * rows, quarter), f32),
            vmem((4 * rows, quarter), bf16),
            pltpu.SemaphoreType.DMA((192,)),
            pltpu.SemaphoreType.DMA((192,)),
            pltpu.SemaphoreType.DMA((96,)),
        ],
        name="fused",
        compiler_params=pltpu.CompilerParams(
            collective_id=1, has_side_effects=True, vmem_limit_bytes=VMEM_LIMIT
        ),
    )(queries, keys, values, tile_mask, out_weight)[0]


def solution(mesh):
    placed = (
        P(("blk", "head"), None),
        P(("blk", "head"), None),
        P(("blk", "head"), None),
        P("head", "blk", None),
        P("head", None),
    )
    return jax.shard_map(
        body, mesh=mesh, in_specs=placed, out_specs=P(("blk", "head"), None), check_vma=False
    )
```

```python
import functools
import math

import jax
import jax.numpy as jnp
from jax import lax
from jax.experimental import pallas as pl
from jax.experimental.pallas import tpu as pltpu
from jax.sharding import PartitionSpec as P

HEAD_DIM = 128
TILE = 128
MESH = pl.DeviceIdType.MESH
TO_LOG2 = math.log2(math.e) / math.sqrt(HEAD_DIM)
LOW = -1e30
BLOCKED = 2e30
VMEM_LIMIT = 60 * 2**20
NX, NY, NZ = 2, 4, 8


def place():
    blk, head = lax.axis_index("blk"), lax.axis_index("head")
    return blk // 16, (blk // 2) % NZ, blk % 2, head // NY, head % NY


def at(x_hi, z, core, x_lo, y):
    return (x_hi * 16 + z * 2 + core, x_lo * NY + y)


def greet(peers):
    barrier = pltpu.get_barrier_semaphore()
    for peer in peers:
        pl.semaphore_signal(barrier, inc=1, device_id=peer, device_id_type=MESH)
    pl.semaphore_wait(barrier, len(peers))


class Wires:
    def __init__(self, send_sems, recv_sems, local_sems):
        self.send_sems, self.recv_sems, self.local_sems = send_sems, recv_sems, local_sems
        self.used, self.used_local = 0, 0
        self.sent = []

    def push(self, src, dst, peer, land=None):
        copy = pltpu.make_async_remote_copy(
            src_ref=src,
            dst_ref=dst,
            send_sem=self.send_sems.at[self.used],
            recv_sem=self.recv_sems.at[self.used],
            device_id=peer,
            device_id_type=MESH,
        )
        arrival = copy
        if land is not None:
            arrival = pltpu.make_async_remote_copy(
                src_ref=land,
                dst_ref=land,
                send_sem=self.send_sems.at[self.used],
                recv_sem=self.recv_sems.at[self.used],
                device_id=peer,
                device_id_type=MESH,
            )
        self.used += 1
        copy.start()
        self.sent.append(copy)
        return arrival

    def local(self, src, dst):
        copy = pltpu.make_async_copy(src, dst, self.local_sems.at[self.used_local])
        self.used_local += 1
        copy.start()
        return copy

    def finish(self):
        for copy in self.sent:
            copy.wait_send()


def fused_kernel(
    q, k, v, m, w,
    out, k_all, v_all, w_all,
    q_here, k_here, v_here, w_here, m_in, bias, query, acc, top_at, total_at,
    o, stat, o_in, stat_in, o_chip, stat_chip, o_far, stat_far, ready, mixed_in, mixed, result,
    send_sems, recv_sems, local_sems,
):
    x_hi, z, core, x_lo, y = place()
    rows = q.shape[0]
    heads, slots, slab = q_here.shape[0], q_here.shape[1], q_here.shape[2]
    width = heads * HEAD_DIM
    row_tiles = slab // TILE
    q_count = slots * slab
    group = x_lo * NY + y
    other_hi, other_core, other_lo = 1 - x_hi, 1 - core, 1 - x_lo
    slot = x_hi * 2 + core
    sibling_slot, across_slot, diagonal_slot = x_hi * 2 + other_core, other_hi * 2 + core, other_hi * 2 + other_core
    sibling = at(x_hi, z, other_core, x_lo, y)
    across = at(other_hi, z, core, x_lo, y)
    diagonal = at(other_hi, z, other_core, x_lo, y)
    z_up, z_down = (z + 1) % NZ, (z + NZ - 1) % NZ
    up, down = at(x_hi, z_up, core, x_lo, y), at(x_hi, z_down, core, x_lo, y)
    y_up, y_down, y_far = (y + 1) % NY, (y + NY - 1) % NY, (y + 2) % NY
    partner = at(x_hi, z, core, other_lo, y)
    outer = at(other_hi, z, core, other_lo, y)
    blk = x_hi * 16 + z * 2 + core
    head_peers = [(group + step) % 8 for step in range(1, 8)]
    neighbour = at(x_hi, z, other_core, x_lo, y + 1 - 2 * (y % 2))
    greet([(blk, peer) for peer in head_peers] + [sibling, across, diagonal, up, down, outer, neighbour])
    wires = Wires(send_sems, recv_sems, local_sems)
    my_rows = pl.ds(pl.multiple_of(group * rows, 64), rows)

    def feature(owner, head):
        return pl.ds(pl.multiple_of(owner * width + head * HEAD_DIM, HEAD_DIM), HEAD_DIM)

    def exchange(src, dst, head):
        arrivals = []
        for step in range(1, 8):
            peer = (group + step) % 8
            origin = (group + 8 - step) % 8
            arrivals.append(
                wires.push(
                    src.at[:, feature(peer, head)],
                    dst.at[my_rows, :],
                    (blk, peer),
                    dst.at[pl.ds(pl.multiple_of(origin * rows, 64), rows), :],
                )
            )
        return arrivals, wires.local(src.at[:, feature(group, head)], dst.at[my_rows, :])

    def settle(pending):
        for arrival in pending[0]:
            arrival.wait_recv()
        pending[1].wait()

    waits = {}

    def exchange_head(head):
        waits["k", head] = exchange(k, k_all.at[head, z], head)
        waits["v", head] = exchange(v, v_all.at[head, z], head)
        waits["q", head] = exchange(q, q_here.at[head, slot], head)

    ring = {}

    def ring_step(full, head, step, direction):
        if direction > 0:
            held, landing, peer = (z + NZ - step) % NZ, (z + NZ - step - 1) % NZ, up
        else:
            held, landing, peer = (z + step) % NZ, (z + step + 1) % NZ, down
        here = full.at[head, held]
        return wires.push(here, here, peer, full.at[head, landing]), landing

    def load(name, head, index):
        if name == "k":
            return wires.local(k_all.at[head, index], k_here.at[head, index])
        return wires.local(v_all.at[head, index], v_here.at[head, index])

    def ring_start(head):
        loading = []
        for name, full in (("k", k_all), ("v", v_all)):
            settle(waits[name, head])
            for direction in (1, -1):
                ring[head, name, direction] = ring_step(full, head, 0, direction)
            loading.append(load(name, head, z))
        return loading

    def ring_turn(head, step):
        loading = []
        for name, full in (("k", k_all), ("v", v_all)):
            for direction in (1, -1):
                last = 4 if (name, direction) in (("k", 1), ("v", -1)) else 3
                if step > last:
                    continue
                arrival, index = ring[head, name, direction]
                arrival.wait_recv()
                if step < last:
                    ring[head, name, direction] = ring_step(full, head, step, direction)
                loading.append(load(name, head, index))
        return loading

    moving = {}

    def queries_out(head):
        settle(waits["q", head])
        mine = q_here.at[head, slot]
        moving["side", head] = wires.push(mine, mine, sibling, q_here.at[head, sibling_slot])
        moving["across", head] = wires.push(mine, mine, across, q_here.at[head, across_slot])

    def queries_on(head):
        moving["across", head].wait_recv()
        theirs = q_here.at[head, across_slot]
        moving["diagonal", head] = wires.push(theirs, theirs, sibling, q_here.at[head, diagonal_slot])

    def queries_in(head):
        moving["side", head].wait_recv()
        moving["diagonal", head].wait_recv()
        for s in range(slots):
            scaled = q_here[head, s].astype(jnp.float32) * TO_LOG2
            coarse = scaled.astype(jnp.bfloat16)
            at_rows = slice(s * slab, (s + 1) * slab)
            query[head, at_rows, :HEAD_DIM] = coarse
            query[head, at_rows, HEAD_DIM:] = (scaled - coarse.astype(jnp.float32)).astype(jnp.bfloat16)

    depth = w.shape[0]
    half = depth // 2
    quarter = w.shape[1] // 4
    parity = y % 2
    y_pair = y + 1 - 2 * parity
    beside = at(x_hi, z, core, x_lo, y_pair)
    mine = pl.ds(pl.multiple_of((parity * 2 + core) * quarter, 128), quarter)
    next_door = pl.ds(pl.multiple_of(((1 - parity) * 2 + core) * quarter, 128), quarter)
    upper, lower = pl.ds(0, half), pl.ds(half, half)

    def w_along(peer_y, from_y, cols):
        return wires.push(w.at[:, cols], w_all.at[group], (blk, x_lo * NY + peer_y), w_all.at[x_lo * NY + from_y])

    def w_cross(yy, own=False):
        arrivals = []
        for part, peer in ((upper, partner), (lower, outer)):
            held = w.at[part, mine] if own else w_all.at[x_lo * NY + yy, part]
            arrivals.append(
                wires.push(held, w_all.at[x_lo * NY + yy, part], peer, w_all.at[other_lo * NY + yy, part])
            )
        return arrivals

    def make_bias(head):
        tile_rows = slots * row_tiles
        spread_rows = lax.broadcasted_iota(jnp.int32, (tile_rows, q_count), 0)
        spread_cols = lax.broadcasted_iota(jnp.int32, (tile_rows, q_count), 1)
        spread = jnp.where(spread_cols // TILE == spread_rows, 1.0, 0.0).astype(jnp.bfloat16)
        allowed = jnp.concatenate([m_in[s, head] for s in range(slots)], axis=0)
        allowed = jnp.where(allowed > 0, 1.0, 0.0).astype(jnp.bfloat16)
        wide = lax.dot_general(allowed, spread, (((0,), (0,)), ((), ())), preferred_element_type=jnp.float32)
        bias[head] = (1.0 - wide) * BLOCKED

    ones = jnp.ones((16, slab), jnp.bfloat16)

    def work(head, loading, first, second=None):
        for one in loading:
            one.wait()

        def one_block(i, unused):
            index = first if second is None else first + i * (second - first)
            key = k_here[head, index]
            scores = lax.dot_general(
                jnp.concatenate([key, key], axis=1),
                query[head],
                (((1,), (1,)), ((), ())),
                preferred_element_type=jnp.float32,
            )
            first_tile = (x_hi * 2 * NZ + index * 2 + core) * row_tiles
            blocked = [bias[head, pl.ds(first_tile + a, 1), :] for a in range(row_tiles)]
            top = top_at[head]
            next_top = top
            for a in range(row_tiles):
                tile_top = jnp.max(scores[a * TILE : (a + 1) * TILE], axis=0, keepdims=True)
                next_top = jnp.maximum(next_top, tile_top - blocked[a])
            weights = jnp.concatenate(
                [
                    jnp.exp2(scores[a * TILE : (a + 1) * TILE] - (next_top + blocked[a])).astype(jnp.bfloat16)
                    for a in range(row_tiles)
                ],
                axis=0,
            )
            shrink = jnp.exp2(top - next_top)
            added = lax.dot_general(
                jnp.concatenate([v_here[head, index].T, ones], axis=0),
                weights,
                (((1,), (0,)), ((), ())),
                preferred_element_type=jnp.float32,
            )
            acc[head] = acc[head] * shrink + added[:HEAD_DIM]
            top_at[head] = next_top
            total_at[head] = total_at[head] * shrink + added[HEAD_DIM : HEAD_DIM + 1]
            return unused

        lax.fori_loop(0, 1 if second is None else 2, one_block, 0)

    def blended(parts):
        best = functools.reduce(jnp.maximum, [st[0:1, :] for _, st in parts])
        shares = [st[1:2, :] * jnp.exp2(st[0:1, :] - best) for _, st in parts]
        total = functools.reduce(jnp.add, shares)
        safe = jnp.maximum(total, 1e-30)
        mean = functools.reduce(
            jnp.add, [part.astype(jnp.float32) * (one / safe) for (part, _), one in zip(parts, shares)]
        )
        return mean, best, total

    def partial_out(head):
        mean = (acc[head] / jnp.maximum(total_at[head], 1e-30)).astype(jnp.bfloat16)
        for s in range(slots):
            cols = slice(s * slab, (s + 1) * slab)
            o[head, s % 2, s // 2] = mean[:, cols]
            stat[head, s % 2, s // 2, 0:1, :] = top_at[head, :, cols]
            stat[head, s % 2, s // 2, 1:2, :] = total_at[head, :, cols]
        return [
            wires.push(o.at[head, other_core], o_in.at[head], sibling, o_in.at[head]),
            wires.push(stat.at[head, other_core], stat_in.at[head], sibling, stat_in.at[head]),
        ]

    def partial_on(head, arrivals):
        for arrival in arrivals:
            arrival.wait_recv()
        for hi in range(2):
            mean, best, total = blended(
                [(o[head, core, hi], stat[head, core, hi]), (o_in[head, hi], stat_in[head, hi])]
            )
            o_chip[head, hi] = mean.astype(jnp.bfloat16)
            stat_chip[head, hi, 0:1, :] = best
            stat_chip[head, hi, 1:2, :] = total
        return [
            wires.push(o_chip.at[head, other_hi], o_far.at[head], across, o_far.at[head]),
            wires.push(stat_chip.at[head, other_hi], stat_far.at[head], across, stat_far.at[head]),
        ]

    def partial_in(head, arrivals):
        for arrival in arrivals:
            arrival.wait_recv()
        mean, _, _ = blended([(o_chip[head, x_hi], stat_chip[head, x_hi]), (o_far[head], stat_far[head])])
        ready[head] = mean.T.astype(jnp.bfloat16)
        my_lanes = pl.ds(pl.multiple_of(group * HEAD_DIM, HEAD_DIM), HEAD_DIM)
        pieces = []
        for step in range(1, 8):
            peer = (group + step) % 8
            origin = (group + 8 - step) % 8
            pieces.append(
                wires.push(
                    ready.at[head, pl.ds(pl.multiple_of(peer // 2 * 2 * rows, 128), 2 * rows), :],
                    mixed_in.at[head, core, :, my_lanes],
                    (blk, peer),
                    mixed_in.at[head, core, :, pl.ds(pl.multiple_of(origin * HEAD_DIM, HEAD_DIM), HEAD_DIM)],
                )
            )
        mixed_in[head, core, :, my_lanes] = ready[head, pl.ds(pl.multiple_of(group // 2 * 2 * rows, 128), 2 * rows), :]
        return pieces

    def share(head, pieces):
        for piece in pieces:
            piece.wait_recv()
        held = mixed_in.at[head, core]
        return wires.push(held, held, sibling, mixed_in.at[head, other_core])

    def project(head, shared):
        shared.wait_recv()
        tokens = mixed_in[head].reshape(4 * rows, 8 * HEAD_DIM)
        part = jnp.dot(tokens, w_here[head], preferred_element_type=jnp.float32)
        if head == 0:
            mixed[...] = part
        elif head < heads - 1:
            mixed[...] += part
        else:
            result[...] = (mixed[...] + part).astype(jnp.bfloat16)

    def pair(step):
        return (z + NZ - step) % NZ, (z + step) % NZ

    exchange_head(0)
    m_wait = [
        wires.push(m, m_in.at[slot], sibling, m_in.at[sibling_slot]),
        wires.push(m, m_in.at[slot], across, m_in.at[across_slot]),
        wires.push(m, m_in.at[slot], diagonal, m_in.at[diagonal_slot]),
    ]
    m_own = wires.local(m, m_in.at[slot])
    own = [ring_start(0)]
    exchange_head(1)
    queries_out(0)
    exchange_head(2)
    own.append(ring_start(1))
    queries_out(1)
    own.append(ring_start(2))
    queries_out(2)
    w_crossed = [w_cross(y, True)]
    w_near = [w_along(y_up, y_down, next_door), w_along(y_down, y_up, next_door)]
    w_far = w_along(y_far, y_far, mine)
    acc[...] = jnp.zeros_like(acc)
    stat[...] = jnp.zeros_like(stat)
    stat_chip[...] = jnp.zeros_like(stat_chip)
    top_at[...] = jnp.full_like(top_at, LOW)
    total_at[...] = jnp.zeros_like(total_at)
    for arrival in m_wait:
        arrival.wait_recv()
    m_own.wait()
    for head in range(heads):
        make_bias(head)

    for head in range(heads):
        queries_on(head)
        turn = ring_turn(head, 1)
        queries_in(head)
        work(head, own[head], z)
        work(head, turn, *pair(1))
    for head in range(heads):
        work(head, ring_turn(head, 2), *pair(2))
    for arrival in w_near:
        arrival.wait_recv()
    w_crossed += [w_cross(y_down), w_cross(y_up)]
    w_far.wait_recv()
    w_crossed.append(w_cross(y_far))
    for head in range(heads):
        work(head, ring_turn(head, 3), *pair(3))
    partial = []
    for head in range(heads - 1):
        work(head, ring_turn(head, 4), (z + 4) % NZ)
        partial.append(partial_out(head))
    turn = ring_turn(heads - 1, 4)
    partial[0] = partial_on(0, partial[0])
    work(heads - 1, turn, (z + 4) % NZ)
    partial.append(partial_out(heads - 1))
    partial[1] = partial_on(1, partial[1])
    pieces = [partial_in(0, partial[0])]
    partial[2] = partial_on(2, partial[2])
    for arrivals in w_crossed:
        for arrival in arrivals:
            arrival.wait_recv()
    w_loads = []
    for head in range(heads):
        band = pl.ds(head * HEAD_DIM, HEAD_DIM)
        for owner, source in [(group, w.at[:, mine])] + [(g, w_all.at[g]) for g in head_peers]:
            to_band = pl.ds(pl.multiple_of(owner * HEAD_DIM, HEAD_DIM), HEAD_DIM)
            w_loads.append(wires.local(source.at[band, :], w_here.at[head, to_band, :]))
    pieces.append(partial_in(1, partial[1]))
    shared = [share(0, pieces[0])]
    pieces.append(partial_in(2, partial[2]))
    shared.append(share(1, pieces[1]))
    for one in w_loads:
        one.wait()
    project(0, shared[0])
    project(1, shared[1])
    shared.append(share(2, pieces[2]))
    project(2, shared[2])

    def result_rows(c, odd):
        return pl.ds(pl.multiple_of((c * 2 + odd) * rows, 64), rows)

    from_core = pl.ds(pl.multiple_of((parity * 2 + other_core) * quarter, 128), quarter)
    from_beside = pl.ds(pl.multiple_of(((1 - parity) * 2 + core) * quarter, 128), quarter)
    from_opposite = pl.ds(pl.multiple_of(((1 - parity) * 2 + other_core) * quarter, 128), quarter)
    returns = [
        wires.push(result.at[result_rows(core, 1 - parity), :], out.at[:, mine], beside, out.at[:, from_beside]),
        wires.push(result.at[result_rows(other_core, 1 - parity), :], out.at[:, mine], neighbour, out.at[:, from_opposite]),
        wires.push(result.at[result_rows(other_core, parity), :], out.at[:, mine], sibling, out.at[:, from_core]),
    ]
    out[:, mine] = result[result_rows(core, parity), :]
    for arrival in returns:
        arrival.wait_recv()
    wires.finish()


def body(queries, keys, values, tile_mask, out_weight):
    rows, features = queries.shape
    heads = tile_mask.shape[0]
    slab, slots = rows * 8, 4
    q_count = slots * slab
    bf16, f32 = jnp.bfloat16, jnp.float32
    hbm = pl.BlockSpec(memory_space=pl.ANY)
    quarter = out_weight.shape[1] // 4
    w_shape = (8, out_weight.shape[0], quarter)
    vmem = pltpu.VMEM
    return pl.pallas_call(
        fused_kernel,
        out_shape=[
            jax.ShapeDtypeStruct(queries.shape, bf16),
            jax.ShapeDtypeStruct((heads, NZ, slab, HEAD_DIM), bf16),
            jax.ShapeDtypeStruct((heads, NZ, slab, HEAD_DIM), bf16),
            jax.ShapeDtypeStruct(w_shape, bf16),
        ],
        in_specs=[hbm] * 5,
        out_specs=[pl.BlockSpec(memory_space=vmem)] + [hbm] * 3,
        scratch_shapes=[
            vmem((heads, slots, slab, HEAD_DIM), bf16),
            vmem((heads, NZ, slab, HEAD_DIM), bf16),
            vmem((heads, NZ, slab, HEAD_DIM), bf16),
            vmem((heads, 8 * HEAD_DIM, quarter), bf16),
            vmem((slots,) + tile_mask.shape, jnp.int32),
            vmem((heads, tile_mask.shape[2], q_count), f32),
            vmem((heads, q_count, 2 * HEAD_DIM), bf16),
            vmem((heads, HEAD_DIM, q_count), f32),
            vmem((heads, 1, q_count), f32),
            vmem((heads, 1, q_count), f32),
            vmem((heads, 2, 2, HEAD_DIM, slab), bf16),
            vmem((heads, 2, 2, 8, slab), f32),
            vmem((heads, 2, HEAD_DIM, slab), bf16),
            vmem((heads, 2, 8, slab), f32),
            vmem((heads, 2, HEAD_DIM, slab), bf16),
            vmem((heads, 2, 8, slab), f32),
            vmem((heads, HEAD_DIM, slab), bf16),
            vmem((heads, 8, slab), f32),
            vmem((heads, slab, HEAD_DIM), bf16),
            vmem((heads, 2, 2 * rows, 8 * HEAD_DIM), bf16),
            vmem((4 * rows, quarter), f32),
            vmem((4 * rows, quarter), bf16),
            pltpu.SemaphoreType.DMA((192,)),
            pltpu.SemaphoreType.DMA((192,)),
            pltpu.SemaphoreType.DMA((96,)),
        ],
        name="fused",
        compiler_params=pltpu.CompilerParams(
            collective_id=1, has_side_effects=True, vmem_limit_bytes=VMEM_LIMIT
        ),
    )(queries, keys, values, tile_mask, out_weight)[0]


def solution(mesh):
    placed = (
        P(("blk", "head"), None),
        P(("blk", "head"), None),
        P(("blk", "head"), None),
        P("head", "blk", None),
        P("head", None),
    )
    return jax.shard_map(
        body, mesh=mesh, in_specs=placed, out_specs=P(("blk", "head"), None), check_vma=False
    )
```
